256 devices in a mesh: pore: 32 (over y, x, core), field: 8 (over z).
Axes of the slice: x: 4, y: 4, z: 8, core: 2. Of those that a mesh axis runs over, the one named last changes fastest.
Arguments:
- rhs: float32 [256, 65536], P('field', 'pore'), may hold values from -24 to 24
- well_ids: int32 [256], P('field'), may hold values from 0 to 65535
- well_weight: float32 [256], P('field'), may hold values from -40 to 40
- pressure: float32 [65536], P('pore'), may hold values from -6 to 6
- shift: float32 [65536], P('pore'), may hold values from 0.05 to 0.5
- conductance: float32 [196608], P('pore'), may hold values from 0.1 to 1
- throat_ends: int32 [2, 196608], P(None, 'pore'), may hold values from 0 to 4095, as said below
- boundary_blocks: int32 [2, 256], P(None, 'pore'), may hold values from 0 to 15, as said below
- boundary_count: int32 [2, 32], P(None, 'pore'), may hold values from 4 to 8, as said below
- jacobi_perm: int32 [65536], P('pore'), may hold values from 0 to 2047, as said below
- jacobi_inverse: bfloat16 [512, 128, 128], P('pore'), as said below
Outputs:
- adjoint: float32 [256, 65536], P('field', 'pore')
- residual: float32 [256, 65536], P('field', 'pore')
- throat_gradient: float32 [196608], P(('pore', 'field'))
The draws below stay inside these ranges and needn't reach their ends.
Inputs may be any that keep to these rules, and one draw needn't show every extreme that they name: `boundary_blocks`: for each partition, row 0 and row 1 each hold 8 distinct indices of its own 128-pore blocks. Only the first boundary_count entries of a partition's row are live; some partition has all 8 of a side live. `throat_ends`: within a partition's 6144 entries, the first 4096 join two different local pores; the next 1024 join a local pore in a live lower-facing block to a live position of the lower partition's upper-facing buffer, the last 1024 likewise upward; each throat between two partitions is listed on both with equal conductance; at the slab's first and last partition the outward entries reach the slab's faces. `jacobi_perm`: for each partition a permutation of its 2048 local pore indices. `jacobi_inverse`: each block is symmetric positive definite.
All inputs are finite; a program needn't handle non-finite values.
Results may differ from the reference program's by a relative error of at most 0.0082.
Values sent between devices are 32-bit elements; how exact they have to be, the bound alone decides.
No kernel may reach another device: no remote copies, remote signals or barrier semaphores. Data moves between devices by JAX's collectives and lax.ppermute only.
A program may use at most 64 MiB of HBM per device.

```python
import math
import jax
import jax.numpy as jnp
from jax import lax

PORES_DEV = 2048
FIELDS = 256
BCOL = 32
BND_BLOCKS = 8
ITERS = 3
PORES = 65536
TH_DEV = 6144
THROATS = 196608
JB_ALL = 512
N_PORE = 32


def network(key):
    buffer_rows = BND_BLOCKS * 128
    jblocks = PORES_DEV // 128
    least_live = max(1, BND_BLOCKS // 2)

    def pick_blocks(subkey):
        return jax.random.permutation(subkey, jblocks)[:BND_BLOCKS].astype(jnp.int32)
    lower_blocks = jax.vmap(pick_blocks)(jax.random.split(jax.random.fold_in(key, 11), N_PORE))
    upper_blocks = jax.vmap(pick_blocks)(jax.random.split(jax.random.fold_in(key, 12), N_PORE))
    lower_count = jax.random.randint(jax.random.fold_in(key, 13), (N_PORE,), least_live, BND_BLOCKS + 1).astype(jnp.int32).at[0].set(BND_BLOCKS)
    upper_count = jax.random.randint(jax.random.fold_in(key, 14), (N_PORE,), least_live, BND_BLOCKS + 1).astype(jnp.int32).at[N_PORE - 1].set(BND_BLOCKS)
    full_count = jnp.full((1,), BND_BLOCKS, jnp.int32)
    below_count = jnp.concatenate([full_count, upper_count])
    above_count = jnp.concatenate([lower_count, full_count])
    extent = (N_PORE + 1, buffer_rows)
    below_slot = jax.random.randint(jax.random.fold_in(key, 15), extent, 0, 1 << 20).astype(jnp.int32) % below_count[:, None]
    below_off = jax.random.randint(jax.random.fold_in(key, 16), extent, 0, 128).astype(jnp.int32)
    above_slot = jax.random.randint(jax.random.fold_in(key, 17), extent, 0, 1 << 20).astype(jnp.int32) % above_count[:, None]
    above_off = jax.random.randint(jax.random.fold_in(key, 18), extent, 0, 128).astype(jnp.int32)
    cross_unit = jax.random.uniform(jax.random.fold_in(key, 19), extent, jnp.float32)
    return {'lower_blocks': lower_blocks, 'upper_blocks': upper_blocks, 'lower_count': lower_count, 'upper_count': upper_count, 'below_slot': below_slot, 'below_off': below_off, 'above_slot': above_slot, 'above_off': above_off, 'cross_unit': cross_unit}


def draw_throat_ends(key, part):
    shared = network(key)
    key = jax.random.fold_in(key, 3)
    buffer_rows = BND_BLOCKS * 128
    near_local = jax.random.randint(jax.random.fold_in(key, 1), (N_PORE, 2 * PORES_DEV), 0, PORES_DEV).astype(jnp.int32)
    step_local = jax.random.randint(jax.random.fold_in(key, 2), (N_PORE, 2 * PORES_DEV), 1, PORES_DEV).astype(jnp.int32)
    far_local = (near_local + step_local) % PORES_DEV
    lower_near = jnp.take_along_axis(shared['lower_blocks'], shared['above_slot'][:N_PORE], axis=1) * 128 + shared['above_off'][:N_PORE]
    lower_far = PORES_DEV + shared['below_slot'][:N_PORE] * 128 + shared['below_off'][:N_PORE]
    upper_near = jnp.take_along_axis(shared['upper_blocks'], shared['below_slot'][1:], axis=1) * 128 + shared['below_off'][1:]
    upper_far = PORES_DEV + buffer_rows + shared['above_slot'][1:] * 128 + shared['above_off'][1:]
    near_all = jnp.concatenate([near_local, lower_near, upper_near], axis=1).reshape(-1)
    far_all = jnp.concatenate([far_local, lower_far, upper_far], axis=1).reshape(-1)
    return jnp.stack([near_all, far_all]).astype(jnp.int32)


def draw_conductance(key, part):
    shared = network(key)
    key = jax.random.fold_in(key, 4)
    local_unit = jax.random.uniform(key, (N_PORE, 2 * PORES_DEV), jnp.float32)
    cross_unit = shared['cross_unit']
    local_vals = jnp.exp(jnp.log(0.1) + local_unit * jnp.log(10.0))
    cross_vals = jnp.exp(jnp.log(0.1) + cross_unit * jnp.log(10.0))
    merged = jnp.concatenate([local_vals, cross_vals[:N_PORE], cross_vals[1:]], axis=1)
    return jnp.clip(merged.reshape(-1), 0.1, 1.0).astype(jnp.float32)


def draw_boundary_blocks(key, part):
    shared = network(key)
    return jnp.stack([shared['lower_blocks'].reshape(-1), shared['upper_blocks'].reshape(-1)]).astype(jnp.int32)


def draw_boundary_count(key, part):
    shared = network(key)
    return jnp.stack([shared['lower_count'], shared['upper_count']]).astype(jnp.int32)


def draw_jacobi_perm(key, part):
    key = jax.random.fold_in(key, 7)

    def local_order(subkey):
        return jax.random.permutation(subkey, PORES_DEV).astype(jnp.int32)
    return jax.vmap(local_order)(jax.random.split(key, N_PORE)).reshape(-1).astype(jnp.int32)


def draw_jacobi_inverse(key, part):
    key = jax.random.fold_in(key, 8)
    diag_key, noise_key = jax.random.split(key)
    diagonal = jax.random.uniform(diag_key, (JB_ALL, 128), jnp.float32, 0.2, 0.5)
    noise = jax.random.normal(noise_key, (JB_ALL, 128, 128), jnp.float32)
    paired = (noise + jnp.swapaxes(noise, 1, 2)) * 0.0042
    identity = jnp.eye(128, dtype=jnp.float32)
    blocks = paired * (1.0 - identity)[None] + identity[None] * diagonal[:, :, None]
    return blocks.astype(jnp.bfloat16)


def draw_rhs(key, part):
    key = jax.random.fold_in(key, 9)
    position = jnp.arange(PORES, dtype=jnp.float32) / PORES
    values = jnp.clip(jax.random.normal(key, (FIELDS, PORES), jnp.float32), -6.0, 6.0) * (1.0 + 2.0 * position)[None, :]
    return values.astype(jnp.float32)


def place_ends(values, rng, least, top_value):
    shape = values.shape
    index_at = [jax.random.randint(jax.random.fold_in(rng, axis), (), 0, shape[axis]) for axis in range(len(shape))]
    values = values.at[tuple(index_at)].set(least)
    longest = shape.index(max(shape))
    index_at[longest] = (index_at[longest] + 1) % shape[longest]
    return values.at[tuple(index_at)].set(top_value)


def level_of(rng, shape, cuts, smallest, top_value):
    factor_of, own = 1.0, jax.random.fold_in(rng, 6)
    for dim, parts in cuts:
        heights = jnp.exp(jax.random.uniform(jax.random.fold_in(own, dim), (parts,), jnp.float32, smallest / len(cuts), top_value / len(cuts)))
        factor_of = factor_of * jnp.repeat(heights, shape[dim] // parts).reshape([-1 if axis == dim else 1 for axis in range(len(shape))])
    return factor_of


def scatter_about(own_key, dims, deviation, limit, shards=(), kind=jnp.bfloat16):
    values = deviation * jax.random.normal(own_key, dims, jnp.float32)
    if shards:
        values = values * level_of(own_key, dims, shards, -0.22, 0.18)
    return jnp.clip(values, -limit, limit).astype(kind)


def setup_inputs(seed: int = 0) -> dict:
    seeds = jax.random.split(jax.random.key(seed), 12)
    rhs = draw_rhs(jax.random.fold_in(seeds[11], 71), 0)
    well_ids = place_ends(jax.random.randint(seeds[1], (FIELDS,), 0, PORES), jax.random.fold_in(seeds[1], 1), 0, PORES - 1).astype(jnp.int32)
    well_weight = scatter_about(seeds[2], (FIELDS,), 8.0, 40.0, ((0, 8),), jnp.float32)
    pressure = scatter_about(seeds[3], (PORES,), 1.0, 6.0, ((0, 32),), jnp.float32)
    shift = jnp.clip(jnp.exp(math.log(0.5) - 2.3025851 * jax.random.uniform(seeds[4], (PORES,), jnp.float32) ** level_of(seeds[4], (PORES,), ((0, 32),), -0.2, 0.2)), 0.05, 0.5)
    conductance = draw_conductance(jax.random.fold_in(seeds[11], 71), 0)
    throat_ends = draw_throat_ends(jax.random.fold_in(seeds[11], 71), 0)
    boundary_blocks = draw_boundary_blocks(jax.random.fold_in(seeds[11], 71), 0)
    boundary_count = draw_boundary_count(jax.random.fold_in(seeds[11], 71), 0)
    jacobi_perm = draw_jacobi_perm(jax.random.fold_in(seeds[11], 71), 0)
    jacobi_inverse = draw_jacobi_inverse(jax.random.fold_in(seeds[11], 71), 0)
    return dict(rhs=rhs, well_ids=well_ids, well_weight=well_weight, pressure=pressure, shift=shift, conductance=conductance, throat_ends=throat_ends, boundary_blocks=boundary_blocks, boundary_count=boundary_count, jacobi_perm=jacobi_perm, jacobi_inverse=jacobi_inverse)


def symmetric(matrix):
    return 0.5 * (matrix + matrix.T)

def solve_small(system, target):
    return jax.scipy.linalg.cho_solve((jnp.linalg.cholesky(system), True), target)

def advance(coeffs, vectors):
    return jnp.einsum('ij,ip->jp', coeffs, vectors, precision=lax.Precision.HIGHEST)

def gram_matrix(former, latter):
    return jnp.einsum('ip,jp->ij', former, latter, precision=lax.Precision.HIGHEST)

def reference(rhs, well_ids, well_weight, pressure, shift, conductance, throat_ends, boundary_blocks, boundary_count, jacobi_perm, jacobi_inverse):
    buffer_rows = BND_BLOCKS * 128
    throat_idx = jnp.arange(THROATS, dtype=jnp.int32)
    partition = throat_idx // TH_DEV
    near_end = throat_ends[0]
    far_end = throat_ends[1]
    inside = far_end < PORES_DEV
    lower_pos = far_end - PORES_DEV
    upper_pos = far_end - PORES_DEV - buffer_rows
    from_lower = (far_end >= PORES_DEV) & (lower_pos < buffer_rows)
    from_upper = upper_pos >= 0
    lower_part = jnp.clip(partition - 1, 0, N_PORE - 1)
    upper_part = jnp.clip(partition + 1, 0, N_PORE - 1)
    lower_slot = jnp.clip(lower_pos // 128, 0, BND_BLOCKS - 1)
    upper_slot = jnp.clip(upper_pos // 128, 0, BND_BLOCKS - 1)
    lower_block = boundary_blocks[1][lower_part * BND_BLOCKS + lower_slot]
    upper_block = boundary_blocks[0][upper_part * BND_BLOCKS + upper_slot]
    lower_live = from_lower & (partition >= 1) & (lower_slot < boundary_count[1][lower_part])
    upper_live = from_upper & (partition + 1 < N_PORE) & (upper_slot < boundary_count[0][upper_part])
    lower_glob = lower_part * PORES_DEV + 128 * lower_block + lower_pos % 128
    upper_glob = upper_part * PORES_DEV + 128 * upper_block + upper_pos % 128
    far_glob = jnp.where(inside, partition * PORES_DEV + far_end, jnp.where(from_lower, lower_glob, upper_glob))
    far_glob = jnp.clip(far_glob, 0, PORES - 1).astype(jnp.int32)
    valid = (inside | lower_live | upper_live).astype(jnp.float32)
    near_glob = (partition * PORES_DEV + near_end).astype(jnp.int32)
    back_glob = jnp.where(inside, far_glob, 0).astype(jnp.int32)
    inside_weight = inside.astype(jnp.float32)

    def operate(values):
        throat_flux = conductance[None, :] * (values[:, near_glob] - values[:, far_glob] * valid[None, :])
        result = shift[None, :] * values
        result = result.at[:, near_glob].add(throat_flux)
        return result.at[:, back_glob].add(-throat_flux * inside_weight[None, :])
    pore_idx = jnp.arange(PORES, dtype=jnp.int32)
    tile_index = (pore_idx // PORES_DEV * PORES_DEV + jacobi_perm).astype(jnp.int32).reshape(JB_ALL, 128)
    inverse_wide = jacobi_inverse.astype(jnp.float32)

    def precondition(values):
        rounded = lax.optimization_barrier(values.astype(jnp.bfloat16))
        pieces = rounded.astype(jnp.float32)[:, tile_index]
        solved = jnp.einsum('cbi,bij->cbj', pieces, inverse_wide, precision=lax.Precision.HIGHEST)
        return jnp.zeros_like(values).at[:, tile_index.reshape(-1)].set(solved.reshape(values.shape[0], -1))
    sources = rhs.at[jnp.arange(FIELDS, dtype=jnp.int32), well_ids].add(well_weight)

    def solve_block(block_sources):
        adjoint = jnp.zeros_like(block_sources)
        residual = block_sources
        smoothed = precondition(residual)
        direction = smoothed
        energy_now = symmetric(gram_matrix(residual, smoothed))
        for iteration in range(ITERS):
            mapped = operate(direction)
            curvature = symmetric(gram_matrix(direction, mapped))
            step_size = solve_small(curvature, energy_now)
            adjoint = adjoint + advance(step_size, direction)
            residual = residual - advance(step_size, mapped)
            if iteration + 1 < ITERS:
                smoothed = precondition(residual)
                energy_next = symmetric(gram_matrix(residual, smoothed))
                mix_coeffs = solve_small(energy_now, energy_next)
                direction = smoothed + advance(mix_coeffs, direction)
                energy_now = energy_next
        return (adjoint, residual)
    adjoint_blocks, residual_blocks = lax.map(solve_block, sources.reshape(FIELDS // BCOL, BCOL, PORES))
    pressure_diff = pressure[near_glob] - pressure[far_glob] * valid

    def block_term(block):
        differences = block[:, near_glob] - block[:, far_glob] * valid[None, :]
        return lax.optimization_barrier(jnp.sum(differences * pressure_diff[None, :], axis=0))
    terms = lax.map(block_term, adjoint_blocks)
    gradient = -(1.0 / math.sqrt(FIELDS)) * lax.optimization_barrier(jnp.sum(terms, axis=0))
    return (adjoint_blocks.reshape(FIELDS, PORES), residual_blocks.reshape(FIELDS, PORES), gradient)
```

```python
import functools
import math

import jax
import jax.numpy as jnp
from jax import lax
from jax.experimental import pallas as pl
from jax.experimental.pallas import tpu as pltpu
from jax.sharding import PartitionSpec as P

FIELDS = 256
BCOL = 32
ITERS = 3
NT = (((1,), (1,)), ((), ()))
NN = (((1,), (0,)), ((), ()))
TN = (((0,), (0,)), ((), ()))
F32 = jnp.float32
BF16 = jnp.bfloat16
CHUNK = 512


def permuted(x, axis, target):
    devices = lax.axis_size(axis)
    pairs = [(i, target(i)) for i in range(devices) if 0 <= target(i) < devices]
    return lax.ppermute(x, axis, pairs)


def pore_sum(x):
    def turned(by, stride):
        def target(i):
            place = (i // stride) % 4
            return i + ((place + by) % 4 - place) * stride

        return target

    x = x + permuted(x, "pore", lambda i: i ^ 1)
    for stride in (2, 8):
        others = [permuted(x, "pore", turned(by, stride)) for by in (1, 2, 3)]
        x = x + others[0] + others[1] + others[2]
    return x


def lane_gather(block, blocks, index):
    shape = block(0).shape
    low = jnp.broadcast_to(index & 127, shape)
    high = jnp.broadcast_to(index >> 7, shape)
    found = jnp.take_along_axis(block(0), low, axis=1)
    for h in range(1, blocks):
        found = jnp.where(high == h, jnp.take_along_axis(block(h), low, axis=1), found)
    return found


def halves(x):
    high = x.astype(BF16)
    low = (x - high.astype(F32)).astype(BF16)
    return high, low


def one_hot(index, value):
    rows = lax.broadcasted_iota(jnp.int32, (256, index.shape[1]), 0)
    return jnp.where(rows == (index & 255), value, 0.0).astype(BF16)


def spread(values, index):
    both = jnp.concatenate(halves(values), axis=0)
    page = index >> 8
    pages = []
    for h in range(8):
        pages.append(both * jnp.where(page == h, 1.0, 0.0).astype(BF16))
    return jnp.concatenate(pages, axis=0)


def page_value(acc_ref, h):
    return acc_ref[h * 64 : h * 64 + 32, :] + acc_ref[h * 64 + 32 : h * 64 + 64, :]


def tile_of(ref, first=0):
    rows = slice(first, first + BCOL)
    return lambda h: ref[rows, h * 128 : (h + 1) * 128]


def apply_inverse(source_ref, perm_ref, inverse_ref, acc_ref, out_ref):
    for chunk in range(4):
        parts = []
        for c in range(4 * chunk, 4 * chunk + 4):
            picked = lane_gather(tile_of(source_ref), 16, perm_ref[0:1, c * 128 : (c + 1) * 128])
            both = jnp.concatenate(halves(picked), axis=0)
            solved = lax.dot_general(both, inverse_ref[c], NN, preferred_element_type=F32)
            parts.append(solved[:BCOL] + solved[BCOL:])
        index = perm_ref[0:1, chunk * 512 : (chunk + 1) * 512]
        part = lax.dot_general(
            spread(jnp.concatenate(parts, axis=1), index),
            one_hot(index, 1.0),
            NT,
            preferred_element_type=F32,
        )
        if chunk == 0:
            acc_ref[...] = part
        else:
            acc_ref[...] += part
    for h in range(8):
        out_ref[:, h * 256 : (h + 1) * 256] = page_value(acc_ref, h)


def fill_sends(values_ref, rows, blocks_ref, count_ref, send_refs, first=0):
    for side, send_ref in enumerate(send_refs):
        for s in range(8):
            start = pl.multiple_of(blocks_ref[side, s] * 128, 128)
            live = jnp.where(s < count_ref[side, 0], 1.0, 0.0)
            send_ref[first : first + rows, s * 128 : (s + 1) * 128] = (
                values_ref[:, pl.ds(start, 128)] * live
            )


def start_kernel(
    blocks_ref, count_ref, rhs_ref, well_ref, weight_ref, perm_ref, inverse_ref, pressure_ref,
    source_ref, smooth_ref, lower_ref, upper_ref, acc_ref,
):
    columns = lax.broadcasted_iota(jnp.int32, rhs_ref.shape, 1)
    source_ref[...] = rhs_ref[...] + jnp.where(columns == well_ref[...], weight_ref[...], 0.0)
    apply_inverse(source_ref, perm_ref, inverse_ref, acc_ref, smooth_ref)
    sends = (lower_ref, upper_ref)
    fill_sends(smooth_ref, BCOL, blocks_ref, count_ref, sends)
    for ref in sends:
        ref[BCOL:, :] = jnp.zeros((8, 1024), F32)
    fill_sends(pressure_ref, 1, blocks_ref, count_ref, sends, BCOL)


def local_kernel(values_ref, ends_ref, cond_ref, shift_ref, out_ref, cross_ref, acc_ref):
    acc_ref[...] = jnp.zeros_like(acc_ref)
    block = tile_of(values_ref)

    def body(i, carry):
        where = pl.ds(pl.multiple_of(i * CHUNK, CHUNK), CHUNK)
        near = ends_ref[0:1, where]
        far = ends_ref[1:2, where]
        drops = []
        for g in range(CHUNK // 128):
            part = slice(g * 128, (g + 1) * 128)
            drops.append(lane_gather(block, 16, near[:, part]) - lane_gather(block, 16, far[:, part]))
        flux = jnp.concatenate(drops, axis=1) * cond_ref[0:1, where]
        left = jnp.concatenate([spread(flux, near), spread(flux, far)], axis=1)
        right = jnp.concatenate([one_hot(near, 1.0), one_hot(far, -1.0)], axis=1)
        acc_ref[...] += lax.dot_general(left, right, NT, preferred_element_type=F32)
        return carry

    lax.fori_loop(0, 4096 // CHUNK, body, 0)
    for g in range(16):
        cross_ref[:, g * 128 : (g + 1) * 128] = lane_gather(
            block, 16, ends_ref[0:1, 4096 + g * 128 : 4096 + (g + 1) * 128]
        )
    for h in range(8):
        part = slice(h * 256, (h + 1) * 256)
        out_ref[:, part] = shift_ref[0:1, part] * values_ref[:, part] + page_value(acc_ref, h)


def add_cross(partial_ref, cross_ref, below_ref, above_ref, ends_ref, cond_ref, acc_ref, out_ref):
    for chunk in range(4):
        ref, base = (below_ref, 2048) if chunk < 2 else (above_ref, 3072)
        drops = []
        for g in range(4 * chunk, 4 * chunk + 4):
            part = slice(4096 + g * 128, 4096 + (g + 1) * 128)
            far = lane_gather(tile_of(ref), 8, ends_ref[1:2, part] - base)
            drops.append(cross_ref[:, g * 128 : (g + 1) * 128] - far)
        part = slice(4096 + chunk * 512, 4096 + (chunk + 1) * 512)
        near = ends_ref[0:1, part]
        flux = jnp.concatenate(drops, axis=1) * cond_ref[0:1, part]
        product = lax.dot_general(
            spread(flux, near), one_hot(near, 1.0), NT, preferred_element_type=F32
        )
        if chunk == 0:
            acc_ref[...] = product
        else:
            acc_ref[...] += product
    for h in range(8):
        part = slice(h * 256, (h + 1) * 256)
        out_ref[:, part] = partial_ref[:, part] + page_value(acc_ref, h)


def step_kernel(
    blocks_ref, count_ref, partial_ref, cross_ref, below_ref, above_ref, ends_ref, cond_ref,
    perm_ref, inverse_ref, mapped_ref, smooth_ref, lower_ref, upper_ref, acc_ref,
):
    add_cross(partial_ref, cross_ref, below_ref, above_ref, ends_ref, cond_ref, acc_ref, mapped_ref)
    apply_inverse(mapped_ref, perm_ref, inverse_ref, acc_ref, smooth_ref)
    fill_sends(smooth_ref, BCOL, blocks_ref, count_ref, (lower_ref, upper_ref))


def exact_dot(a, b, dims):
    return lax.dot_general(a, b, dims, precision=lax.Precision.HIGHEST, preferred_element_type=F32)


def last_kernel(
    partial_ref, cross_ref, below_ref, above_ref, ends_ref, cond_ref,
    z0_ref, z1_ref, z2_ref, q0_ref, q1_ref, source_ref, mapped_ref, gram_ref, acc_ref,
):
    add_cross(partial_ref, cross_ref, below_ref, above_ref, ends_ref, cond_ref, acc_ref, mapped_ref)
    smooth = jnp.concatenate([z0_ref[...], z1_ref[...], z2_ref[...]], axis=0)
    mapped = jnp.concatenate([q0_ref[...], q1_ref[...], mapped_ref[...], source_ref[...]], axis=0)
    gram_ref[...] = exact_dot(smooth, mapped, NT)


def solve_kernel(
    gram_ref, z0_ref, z1_ref, z2_ref, b0_ref, b1_ref, b2_ref, a0_ref, a1_ref, a2_ref,
    pressure_ref, ends_ref, coeff_ref, term_ref, row_ref,
):
    gram = gram_ref[...]
    square = gram[:, :96]
    table = jnp.concatenate([0.5 * (square + square.T), gram[:, 96:]], axis=1)
    row_at = lax.broadcasted_iota(jnp.int32, table.shape, 0)
    for j in range(96):
        pivot = table[j : j + 1, :] / table[j : j + 1, j : j + 1]
        table = jnp.where(row_at == j, pivot, table - table[:, j : j + 1] * pivot)
    coeff = table[:, 96:]
    coeff_ref[...] = coeff
    weight = jnp.broadcast_to(jnp.sum(coeff, axis=1, keepdims=True), (96, 8))
    for place, refs in ((0, (z0_ref, z1_ref, z2_ref)), (2048, (b0_ref, b1_ref, b2_ref)), (3072, (a0_ref, a1_ref, a2_ref))):
        values = jnp.concatenate([ref[:BCOL, :] for ref in refs], axis=0)
        row_ref[0:8, place : place + values.shape[1]] = exact_dot(weight, values, TN)
    row_ref[8:16, 0:2048] = jnp.broadcast_to(pressure_ref[0:1, :], (8, 2048))
    row_ref[8:16, 2048:3072] = jnp.broadcast_to(b0_ref[BCOL : BCOL + 1, :], (8, 1024))
    row_ref[8:16, 3072:4096] = jnp.broadcast_to(a0_ref[BCOL : BCOL + 1, :], (8, 1024))

    def block_from(first, offset):
        return lambda h: row_ref[first : first + 8, offset + h * 128 : offset + (h + 1) * 128]

    for v in range(6):
        near, far = (
            jnp.concatenate(
                [ends_ref[e : e + 1, (8 * v + j) * 128 : (8 * v + j + 1) * 128] for j in range(8)],
                axis=0,
            )
            for e in (0, 1)
        )
        offset, blocks = ((0, 16), (2048, 8), (3072, 8))[max(v - 3, 0)]
        drops = [
            lane_gather(block_from(first, 0), 16, near)
            - lane_gather(block_from(first, offset), blocks, far - offset)
            for first in (0, 8)
        ]
        term_ref[8 * v : 8 * v + 8, :] = drops[0] * drops[1] * (-1.0 / math.sqrt(FIELDS))


def finish_kernel(
    coeff_ref, z0_ref, z1_ref, z2_ref, q0_ref, q1_ref, q2_ref, source_ref, adjoint_ref, residual_ref
):
    coeff = coeff_ref[...]
    smooth = jnp.concatenate([z0_ref[...], z1_ref[...], z2_ref[...]], axis=0)
    mapped = jnp.concatenate([q0_ref[...], q1_ref[...], q2_ref[...]], axis=0)
    adjoint_ref[...] = exact_dot(coeff, smooth, TN)
    residual_ref[...] = source_ref[...] - exact_dot(coeff, mapped, TN)


def call(kernel, scalars, tensors, outs, scratch, name, flops=0):
    shapes = [jax.ShapeDtypeStruct(s, F32) for s in outs]
    return pl.pallas_call(
        kernel,
        out_shape=shapes,
        in_specs=[pl.BlockSpec(memory_space=pltpu.SMEM)] * len(scalars)
        + [pl.BlockSpec(memory_space=pltpu.VMEM)] * len(tensors),
        out_specs=[pl.BlockSpec(memory_space=pltpu.VMEM)] * len(outs),
        scratch_shapes=scratch,
        compiler_params=pltpu.CompilerParams(vmem_limit_bytes=32 << 20),
        cost_estimate=pl.CostEstimate(flops=flops, bytes_accessed=2 << 20, transcendentals=0),
        name=name,
    )(*scalars, *tensors)


def shards(
    rhs, well_ids, well_weight, pressure, shift, conductance, throat_ends, boundary_blocks,
    boundary_count, jacobi_perm, jacobi_inverse,
):
    pores = rhs.shape[1]
    well = (well_ids - lax.axis_index("pore") * pores)[:, None]
    weight = well_weight[:, None]
    perm = jacobi_perm[None, :]
    pressure_row = pressure[None, :]
    shift_row = shift[None, :]
    cond = conductance[None, :]
    scalars = (boundary_blocks, boundary_count)
    field = (BCOL, pores)
    sent = (BCOL, 1024)
    acc = [pltpu.VMEM((512, 256), F32)]
    work = 12 * 10**9

    source, z, lower, upper = call(
        start_kernel, scalars,
        (rhs, well, weight, perm, jacobi_inverse, pressure_row),
        (field, field, (40, 1024), (40, 1024)), acc, "start",
    )
    smooths, mappeds, belows, aboves = [], [], [], []
    for k in range(ITERS):
        below = permuted(upper, "pore", lambda i: i + 1)
        above = permuted(lower, "pore", lambda i: i - 1)
        partial, cross = call(
            local_kernel, (), (z, throat_ends, cond, shift_row),
            (field, field), acc, "local", work,
        )
        smooths.append(z)
        belows.append(below)
        aboves.append(above)
        met = (partial, cross, below, above, throat_ends, cond)
        if k + 1 < ITERS:
            mapped, z, lower, upper = call(
                step_kernel, scalars, met + (perm, jacobi_inverse),
                (field, field, sent, sent), acc, "step",
            )
        else:
            mapped, gram = call(
                last_kernel, (), met + (*smooths, *mappeds, source),
                (field, (96, 128)), acc, "last",
            )
        mappeds.append(mapped)
    gram = pore_sum(gram)
    coeff, term = call(
        solve_kernel, (), (gram, *smooths, *belows, *aboves, pressure_row, throat_ends),
        ((96, BCOL), (48, 128)), [pltpu.VMEM((16, 4096), F32)], "solve",
    )
    shared = lax.all_to_all(term, "field", 0, 0, tiled=True)
    adjoint, residual = call(
        finish_kernel, (), (coeff, *smooths, *mappeds, source), (field, field), [], "finish", work,
    )
    gradient = jnp.sum(shared.reshape(8, -1), axis=0)
    return (adjoint, residual, gradient)


def solution(mesh):
    in_specs = (
        P("field", "pore"),
        P("field"),
        P("field"),
        P("pore"),
        P("pore"),
        P("pore"),
        P(None, "pore"),
        P(None, "pore"),
        P(None, "pore"),
        P("pore"),
        P("pore", None, None),
    )
    out_specs = (P("field", "pore"), P("field", "pore"), P(("pore", "field")))
    return jax.shard_map(shards, mesh=mesh, in_specs=in_specs, out_specs=out_specs, check_vma=False)
```

```python
import functools
import math

import jax
import jax.numpy as jnp
from jax import lax
from jax.experimental import pallas as pl
from jax.experimental.pallas import tpu as pltpu
from jax.sharding import PartitionSpec as P

FIELDS = 256
BCOL = 32
ITERS = 3
NT = (((1,), (1,)), ((), ()))
NN = (((1,), (0,)), ((), ()))
TN = (((0,), (0,)), ((), ()))
F32 = jnp.float32
BF16 = jnp.bfloat16
CHUNK = 512
PANEL = 4


def permuted(x, axis, target):
    devices = lax.axis_size(axis)
    pairs = [(i, target(i)) for i in range(devices) if 0 <= target(i) < devices]
    return lax.ppermute(x, axis, pairs)


def pore_sum(copies):
    chips = copies.shape[0]
    groups = [[2 * chip + core for chip in range(chips)] for core in range(2)]
    received = lax.all_to_all(copies, "pore", 0, 0, axis_index_groups=groups, tiled=True)
    mine = jnp.sum(received, axis=0)
    return mine, permuted(mine, "pore", lambda i: i ^ 1)


def swapped_faces(even_face, odd_face):
    inner = permuted(even_face, "pore", lambda i: i ^ 1)
    outer = permuted(odd_face, "pore", lambda i: ((i + 1) ^ 1) - 1)
    return inner, outer


def is_odd():
    return lax.axis_index("pore") % 2 == 1


def lane_gather(block, blocks, index):
    shape = block(0).shape
    low = jnp.broadcast_to(index & 127, shape)
    high = jnp.broadcast_to(index >> 7, shape)
    found = jnp.take_along_axis(block(0), low, axis=1)
    for h in range(1, blocks):
        found = jnp.where(high == h, jnp.take_along_axis(block(h), low, axis=1), found)
    return found


def halves(x):
    high = x.astype(BF16)
    low = (x - high.astype(F32)).astype(BF16)
    return high, low


def one_hot(index, value):
    rows = lax.broadcasted_iota(jnp.int32, (256, index.shape[1]), 0)
    return jnp.where(rows == (index & 255), value, 0.0).astype(BF16)


def page_table(values_ref, table_ref):
    for h in range(8):
        high, low = halves(values_ref[:, h * 256 : (h + 1) * 256])
        table_ref[h * 64 : h * 64 + 32, :] = high
        table_ref[h * 64 + 32 : h * 64 + 64, :] = low


def page_gather(table_ref, index):
    found = lax.dot_general(table_ref[...], one_hot(index, 1.0), NN, preferred_element_type=F32)
    pages = [found[h * 64 : h * 64 + 32] + found[h * 64 + 32 : h * 64 + 64] for h in range(8)]
    page = jnp.broadcast_to(index >> 8, pages[0].shape)
    picked = pages[0]
    for h in range(1, 8):
        picked = jnp.where(page == h, pages[h], picked)
    return picked


def spread(values, index):
    both = jnp.concatenate(halves(values), axis=0)
    page = index >> 8
    pages = []
    for h in range(8):
        pages.append(both * jnp.where(page == h, 1.0, 0.0).astype(BF16))
    return jnp.concatenate(pages, axis=0)


def page_value(acc_ref, h):
    return acc_ref[h * 64 : h * 64 + 32, :] + acc_ref[h * 64 + 32 : h * 64 + 64, :]


def tile_of(ref, first=0):
    rows = slice(first, first + BCOL)
    return lambda h: ref[rows, h * 128 : (h + 1) * 128]


def apply_inverse(source_ref, perm_ref, inverse_ref, acc_ref, out_ref):
    for chunk in range(4):
        parts = []
        for c in range(4 * chunk, 4 * chunk + 4):
            picked = lane_gather(tile_of(source_ref), 16, perm_ref[0:1, c * 128 : (c + 1) * 128])
            both = jnp.concatenate(halves(picked), axis=0)
            solved = lax.dot_general(both, inverse_ref[c], NN, preferred_element_type=F32)
            parts.append(solved[:BCOL] + solved[BCOL:])
        index = perm_ref[0:1, chunk * 512 : (chunk + 1) * 512]
        part = lax.dot_general(
            spread(jnp.concatenate(parts, axis=1), index),
            one_hot(index, 1.0),
            NT,
            preferred_element_type=F32,
        )
        if chunk == 0:
            acc_ref[...] = part
        else:
            acc_ref[...] += part
    for h in range(8):
        out_ref[:, h * 256 : (h + 1) * 256] = page_value(acc_ref, h)


def fill_sends(values_ref, rows, blocks_ref, count_ref, send_refs, first=0):
    odd = jnp.where(is_odd(), 1, 0)
    for side, send_ref in zip((1 - odd, odd), send_refs):
        for s in range(8):
            start = pl.multiple_of(blocks_ref[side, s] * 128, 128)
            live = jnp.where(s < count_ref[0, side], 1.0, 0.0)
            send_ref[first : first + rows, s * 128 : (s + 1) * 128] = (
                values_ref[:, pl.ds(start, 128)] * live
            )


def start_kernel(
    blocks_hbm, count_hbm, ids_hbm, weight_hbm, rhs_hbm, perm_hbm, inverse_hbm, pressure_hbm,
    source_ref, smooth_ref, inner_ref, outer_ref,
    acc_ref, blocks_ref, count_ref, ids_ref, weight_ref, perm_ref, inverse_ref, pressure_ref, sems,
):
    pairs = (
        (rhs_hbm, source_ref),
        (inverse_hbm, inverse_ref),
        (ids_hbm, ids_ref),
        (weight_hbm, weight_ref),
        (perm_hbm, perm_ref),
        (blocks_hbm, blocks_ref),
        (count_hbm, count_ref),
        (pressure_hbm, pressure_ref),
    )
    copies = [pltpu.make_async_copy(src, dst, sems.at[n]) for n, (src, dst) in enumerate(pairs)]
    for copy in copies:
        copy.start()
    for copy in copies:
        copy.wait()
    first_pore = lax.axis_index("pore") * source_ref.shape[1]
    lanes = lax.broadcasted_iota(jnp.int32, (1, 128), 1)
    for f in range(BCOL):
        place = ids_ref[f] - first_pore
        inside = (place >= 0) & (place < source_ref.shape[1])
        place = jnp.where(inside, place, 0)
        tile = pl.ds(pl.multiple_of((place >> 7) * 128, 128), 128)
        added = jnp.where(inside, weight_ref[f], 0.0)
        source_ref[f : f + 1, tile] += jnp.where(lanes == (place & 127), added, 0.0)
    apply_inverse(source_ref, perm_ref, inverse_ref, acc_ref, smooth_ref)
    sends = (inner_ref, outer_ref)
    fill_sends(smooth_ref, BCOL, blocks_ref, count_ref, sends)
    for ref in sends:
        ref[BCOL:, :] = jnp.zeros((8, 1024), F32)
    fill_sends(pressure_ref, 1, blocks_ref, count_ref, sends, BCOL)


def local_kernel(
    values_ref, ends_ref, cond_ref, shift_ref, out_ref, cross_ref, acc_ref, table_ref
):
    block = tile_of(values_ref)
    page_table(values_ref, table_ref)

    def flux_of(part):
        near = page_gather(table_ref, ends_ref[0:1, part])
        far = [
            lane_gather(block, 16, ends_ref[1:2, g : g + 128])
            for g in range(part.start, part.stop, 128)
        ]
        return (near - jnp.concatenate(far, axis=1)) * cond_ref[0:1, part]

    def scattered(flux, part):
        near = ends_ref[0:1, part]
        far = ends_ref[1:2, part]
        left = jnp.concatenate([spread(flux, near), spread(flux, far)], axis=1)
        right = jnp.concatenate([one_hot(near, 1.0), one_hot(far, -1.0)], axis=1)
        return lax.dot_general(left, right, NT, preferred_element_type=F32)

    parts = [slice(start, start + CHUNK) for start in range(0, 4096, CHUNK)]
    flux = flux_of(parts[0])
    for n, part in enumerate(parts):
        later = flux_of(parts[n + 1]) if n + 1 < len(parts) else None
        if n == 0:
            acc_ref[...] = scattered(flux, part)
        else:
            acc_ref[...] += scattered(flux, part)
        flux = later
    for start in range(0, 2048, CHUNK):
        index = ends_ref[0:1, 4096 + start : 4096 + start + CHUNK]
        cross_ref[:, start : start + CHUNK] = page_gather(table_ref, index)
    for h in range(8):
        part = slice(h * 256, (h + 1) * 256)
        out_ref[:, part] = shift_ref[0:1, part] * values_ref[:, part] + page_value(acc_ref, h)


def add_cross(
    partial_ref, cross_ref, inner_ref, outer_ref, ends_ref, cond_ref, acc_ref, face_ref, out_ref
):
    odd = is_odd()
    inner = inner_ref[:BCOL, :]
    outer = outer_ref[:BCOL, :]
    face_ref[0] = jnp.where(odd, inner, outer)
    face_ref[1] = jnp.where(odd, outer, inner)
    for chunk in range(4):
        ref, base = face_ref.at[chunk // 2], 2048 + chunk // 2 * 1024
        drops = []
        for g in range(4 * chunk, 4 * chunk + 4):
            part = slice(4096 + g * 128, 4096 + (g + 1) * 128)
            far = lane_gather(tile_of(ref), 8, ends_ref[1:2, part] - base)
            drops.append(cross_ref[:, g * 128 : (g + 1) * 128] - far)
        part = slice(4096 + chunk * 512, 4096 + (chunk + 1) * 512)
        near = ends_ref[0:1, part]
        flux = jnp.concatenate(drops, axis=1) * cond_ref[0:1, part]
        product = lax.dot_general(
            spread(flux, near), one_hot(near, 1.0), NT, preferred_element_type=F32
        )
        if chunk == 0:
            acc_ref[...] = product
        else:
            acc_ref[...] += product
    for h in range(8):
        part = slice(h * 256, (h + 1) * 256)
        out_ref[:, part] = partial_ref[:, part] + page_value(acc_ref, h)


def step_kernel(
    blocks_ref, count_ref, partial_ref, cross_ref, inner_ref, outer_ref, ends_ref, cond_ref,
    perm_ref, inverse_ref, mapped_ref, smooth_ref, inner_send, outer_send, acc_ref, face_ref,
):
    add_cross(
        partial_ref, cross_ref, inner_ref, outer_ref, ends_ref, cond_ref, acc_ref, face_ref, mapped_ref
    )
    apply_inverse(mapped_ref, perm_ref, inverse_ref, acc_ref, smooth_ref)
    fill_sends(smooth_ref, BCOL, blocks_ref, count_ref, (inner_send, outer_send))


def exact_dot(a, b, dims):
    return lax.dot_general(a, b, dims, precision=lax.Precision.HIGHEST, preferred_element_type=F32)


def square_index():
    return (lax.broadcasted_iota(jnp.int32, (BCOL, BCOL), axis) for axis in (0, 1))


def packed(moments):
    row, column = square_index()
    pairs, diagonals = [], []
    for upper, lower in zip(moments[::2], moments[1::2]):
        pairs.append(jnp.where(row <= column, upper, lower))
        diagonals.append(jnp.sum(jnp.where(row == column, lower, 0.0), axis=0, keepdims=True))
    diagonals.append(jnp.zeros((BCOL - 3, BCOL), F32))
    return jnp.concatenate(pairs + [jnp.concatenate(diagonals, axis=0)], axis=1)


def unpacked(table):
    row, column = square_index()
    turned = table.T
    moments = []
    for n in range(3):
        pair = table[:, BCOL * n : BCOL * (n + 1)]
        mirror = turned[BCOL * n : BCOL * (n + 1), :]
        diagonal = table[n : n + 1, 3 * BCOL :]
        moments.append(jnp.where(row <= column, pair, mirror))
        outside = jnp.where(row > column, pair, mirror)
        moments.append(jnp.where(row == column, diagonal, outside))
    return moments


def last_kernel(
    partial_ref, cross_ref, inner_ref, outer_ref, ends_ref, cond_ref,
    z0_ref, z1_ref, z2_ref, q0_ref, q1_ref, source_ref, mapped_ref, moment_ref, acc_ref, face_ref,
):
    add_cross(
        partial_ref, cross_ref, inner_ref, outer_ref, ends_ref, cond_ref, acc_ref, face_ref, mapped_ref
    )
    smooth = jnp.concatenate([z0_ref[...], z1_ref[...], z2_ref[...]], axis=0)
    mapped = jnp.concatenate([q0_ref[...], q1_ref[...], mapped_ref[...], source_ref[...]], axis=0)
    products = lax.dot_general(
        jnp.concatenate(halves(smooth), axis=0),
        jnp.concatenate(halves(mapped), axis=0),
        NT,
        preferred_element_type=F32,
    )
    gram = products[:96] + products[96:]
    gram = gram[:, :128] + gram[:, 128:]
    z0, z1, z2 = gram[:32], gram[32:64], gram[64:]
    moments = packed(
        (z0[:, 96:], z0[:, :32], z1[:, :32], z1[:, 32:64], z2[:, 32:64], z2[:, 64:96])
    )
    for n in range(moment_ref.shape[0]):
        moment_ref[n] = moments


def solved_table(table):
    tiles = [table[8 * v : 8 * v + 8, :] for v in range(12)]
    row_at = lax.broadcasted_iota(jnp.int32, (8, 128), 0)
    for first in range(0, 96, PANEL):
        columns = [
            [jnp.broadcast_to(tile[:, first + q : first + q + 1], (8, 128)) for tile in tiles]
            for q in range(PANEL)
        ]
        for p in range(PANEL):
            v, r = divmod(first + p, 8)
            inverse = 1.0 / columns[p][v][r : r + 1, :]
            row = tiles[v][r : r + 1, :] * inverse
            factors = [columns[q][v][r : r + 1, :] * inverse for q in range(p + 1, PANEL)]
            for u in range(12):
                column = columns[p][u]
                tiles[u] = tiles[u] - column * row
                for q, factor in zip(range(p + 1, PANEL), factors):
                    columns[q][u] = columns[q][u] - column * factor
            tiles[v] = jnp.where(row_at == r, row, tiles[v])
            for q, factor in zip(range(p + 1, PANEL), factors):
                columns[q][v] = jnp.where(row_at == r, factor, columns[q][v])
    return tiles


def ends_tile(ends_ref, end, v):
    rows = [ends_ref[end : end + 1, j * 128 : (j + 1) * 128] for j in range(8 * v, 8 * v + 8)]
    return jnp.concatenate(rows, axis=0)


def throat_drop(row_ref, ends_ref, v):
    def block_at(offset):
        return lambda h: row_ref[:, offset + h * 128 : offset + (h + 1) * 128]

    offset, blocks = ((0, 16), (2048, 8), (3072, 8))[max(v - 3, 0)]
    near = lane_gather(block_at(0), 16, ends_tile(ends_ref, 0, v))
    return near - lane_gather(block_at(offset), blocks, ends_tile(ends_ref, 1, v) - offset)


def place_faces(row_ref, inner, outer):
    odd = is_odd()
    row_ref[:, 2048:3072] = jnp.broadcast_to(jnp.where(odd, inner, outer), (8, 1024))
    row_ref[:, 3072:4096] = jnp.broadcast_to(jnp.where(odd, outer, inner), (8, 1024))


def pressure_kernel(pressure_ref, inner_ref, outer_ref, ends_ref, drop_ref, row_ref):
    row_ref[:, 0:2048] = jnp.broadcast_to(pressure_ref[0:1, :], (8, 2048))
    place_faces(row_ref, inner_ref[BCOL : BCOL + 1, :], outer_ref[BCOL : BCOL + 1, :])
    for v in range(6):
        drop = throat_drop(row_ref, ends_ref, v)
        drop_ref[8 * v : 8 * v + 8, :] = drop * (-1.0 / math.sqrt(FIELDS))


def solve_kernel(
    mine_ref, other_ref, z0_ref, z1_ref, z2_ref, i0_ref, i1_ref, i2_ref, o0_ref, o1_ref, o2_ref,
    drop_ref, ends_ref, coeff_ref, term_ref, row_ref, total_ref,
):
    m = unpacked(mine_ref[...] + other_ref[...])
    rows = [jnp.concatenate([m[n + 1], m[n + 2], m[n + 3], m[n]], axis=1) for n in range(3)]
    tiles = solved_table(jnp.concatenate(rows, axis=0))
    for v in range(12):
        coeff_ref[8 * v : 8 * v + 8, :] = tiles[v][:, 96:]
    weights = [
        jnp.broadcast_to(jnp.sum(tile[:, 96:], axis=1, keepdims=True), (8, 128)) for tile in tiles
    ]

    def weighted(refs, start):
        part = slice(start, start + 128)
        total = None
        for v in range(12):
            ref = refs[v // 4]
            product = weights[v] * ref[8 * (v % 4) : 8 * (v % 4) + 8, part]
            total = product if total is None else total + product
        return jnp.sum(total, axis=0, keepdims=True)

    for start in range(0, 2048, 128):
        row_ref[:, start : start + 128] = jnp.broadcast_to(
            weighted((z0_ref, z1_ref, z2_ref), start), (8, 128)
        )
    inner, outer = (
        jnp.concatenate([weighted(refs, start) for start in range(0, 1024, 128)], axis=1)
        for refs in ((i0_ref, i1_ref, i2_ref), (o0_ref, o1_ref, o2_ref))
    )
    place_faces(row_ref, inner, outer)
    for v in range(6):
        drop = throat_drop(row_ref, ends_ref, v)
        total_ref[8 * v : 8 * v + 8, :] = drop * drop_ref[8 * v : 8 * v + 8, :]
    for n in range(8):
        term_ref[n] = total_ref[6 * n : 6 * n + 6, :]


def finish_kernel(
    coeff_ref, z0_ref, z1_ref, z2_ref, q0_ref, q1_ref, q2_ref, source_ref, adjoint_ref, residual_ref
):
    coeff = coeff_ref[...]
    smooth = jnp.concatenate([z0_ref[...], z1_ref[...], z2_ref[...]], axis=0)
    mapped = jnp.concatenate([q0_ref[...], q1_ref[...], q2_ref[...]], axis=0)
    adjoint_ref[...] = exact_dot(coeff, smooth, TN)
    residual_ref[...] = source_ref[...] - exact_dot(coeff, mapped, TN)


def call(kernel, spaces, args, outs, scratch, name, flops=0):
    return pl.pallas_call(
        kernel,
        out_shape=[jax.ShapeDtypeStruct(s, F32) for s in outs],
        in_specs=[pl.BlockSpec(memory_space=space) for space in spaces],
        out_specs=[pl.BlockSpec(memory_space=pltpu.VMEM)] * len(outs),
        scratch_shapes=scratch,
        compiler_params=pltpu.CompilerParams(vmem_limit_bytes=32 << 20),
        cost_estimate=pl.CostEstimate(flops=flops, bytes_accessed=2 << 20, transcendentals=0),
        name=name,
    )(*args)


def shards(
    rhs, well_ids, well_weight, pressure, shift, conductance, throat_ends, boundary_blocks,
    boundary_count, jacobi_perm, jacobi_inverse,
):
    pores = rhs.shape[1]
    perm = jacobi_perm[None, :]
    pressure_row = pressure[None, :]
    shift_row = shift[None, :]
    cond = conductance[None, :]
    field = (BCOL, pores)
    sent = (BCOL, 1024)
    smem, vmem = pltpu.SMEM, pltpu.VMEM
    acc = pltpu.VMEM((512, 256), F32)
    table = pltpu.VMEM((512, 256), BF16)
    face = pltpu.VMEM((2, *sent), F32)
    work = 12 * 10**9

    counts = boundary_count.T
    chips = lax.axis_size("pore") // 2
    source, z, *sends = call(
        start_kernel, [pltpu.HBM] * 8,
        (boundary_blocks, counts, well_ids, well_weight, rhs, perm, jacobi_inverse, pressure_row),
        (field, field, (40, 1024), (40, 1024)),
        [
            acc, smem(boundary_blocks.shape, jnp.int32), smem(counts.shape, jnp.int32),
            smem(well_ids.shape, jnp.int32), smem(well_weight.shape, F32),
            vmem(perm.shape, jnp.int32), vmem(jacobi_inverse.shape, BF16), vmem(perm.shape, F32),
            pltpu.SemaphoreType.DMA((8,)),
        ],
        "start",
    )
    smooths, mappeds, inners, outers = [], [], [], []
    for k in range(ITERS):
        inner, outer = swapped_faces(*sends)
        partial, cross = call(
            local_kernel, [vmem] * 4, (z, throat_ends, cond, shift_row),
            (field, field), [acc, table], "local", work,
        )
        smooths.append(z)
        inners.append(inner)
        outers.append(outer)
        met = (partial, cross, inner, outer, throat_ends, cond)
        if k + 1 < ITERS:
            mapped, z, *sends = call(
                step_kernel, [smem] * 2 + [vmem] * 8,
                (boundary_blocks, counts, *met, perm, jacobi_inverse),
                (field, field, sent, sent), [acc, face], "step",
            )
        else:
            mapped, moments = call(
                last_kernel, [vmem] * 12, met + (*smooths, *mappeds, source),
                (field, (chips, BCOL, 128)), [acc, face], "last",
            )
        mappeds.append(mapped)
    mine, other = pore_sum(moments)
    row = pltpu.VMEM((8, 4096), F32)
    (drop,) = call(
        pressure_kernel, [vmem] * 4, (pressure_row, inners[0], outers[0], throat_ends),
        ((48, 128),), [row], "pressure", work,
    )
    coeff, term = call(
        solve_kernel, [vmem] * 13, (mine, other, *smooths, *inners, *outers, drop, throat_ends),
        ((96, BCOL), (8, 6, 128)), [row, pltpu.VMEM((48, 128), F32)], "solve",
    )
    shared = lax.all_to_all(term, "field", 0, 0, tiled=True)
    adjoint, residual = call(
        finish_kernel, [vmem] * 8, (coeff, *smooths, *mappeds, source), (field, field), [],
        "finish", work,
    )
    gradient = jnp.sum(shared, axis=0).reshape(-1)
    return (adjoint, residual, gradient)


def solution(mesh):
    in_specs = (
        P("field", "pore"),
        P("field"),
        P("field"),
        P("pore"),
        P("pore"),
        P("pore"),
        P(None, "pore"),
        P(None, "pore"),
        P(None, "pore"),
        P("pore"),
        P("pore", None, None),
    )
    out_specs = (P("field", "pore"), P("field", "pore"), P(("pore", "field")))
    return jax.shard_map(shards, mesh=mesh, in_specs=in_specs, out_specs=out_specs, check_vma=False)
```

```python
import functools
import math

import jax
import jax.numpy as jnp
from jax import lax
from jax.experimental import pallas as pl
from jax.experimental.pallas import tpu as pltpu
from jax.sharding import PartitionSpec as P

FIELDS = 256
BCOL = 32
ITERS = 3
NT = (((1,), (1,)), ((), ()))
NN = (((1,), (0,)), ((), ()))
TN = (((0,), (0,)), ((), ()))
F32 = jnp.float32
BF16 = jnp.bfloat16
CHUNK = 512
SIDE = 16


def permuted(x, axis, target):
    devices = lax.axis_size(axis)
    pairs = [(i, target(i)) for i in range(devices) if 0 <= target(i) < devices]
    return lax.ppermute(x, axis, pairs)


def pore_sum(copies):
    chips = copies.shape[0]
    groups = [[2 * chip + core for chip in range(chips)] for core in range(2)]
    received = lax.all_to_all(copies, "pore", 0, 0, axis_index_groups=groups, tiled=True)
    mine = jnp.sum(received, axis=0)
    return mine, permuted(mine, "pore", lambda i: i ^ 1)


def swapped_faces(even_face, odd_face):
    inner = permuted(even_face, "pore", lambda i: i ^ 1)
    outer = permuted(odd_face, "pore", lambda i: ((i + 1) ^ 1) - 1)
    return inner, outer


def is_odd():
    return lax.axis_index("pore") % 2 == 1


def lane_gather(block, blocks, index):
    shape = block(0).shape
    low = jnp.broadcast_to(index & 127, shape)
    high = jnp.broadcast_to(index >> 7, shape)
    found = jnp.take_along_axis(block(0), low, axis=1)
    for h in range(1, blocks):
        found = jnp.where(high == h, jnp.take_along_axis(block(h), low, axis=1), found)
    return found


def halves(x):
    high = x.astype(BF16)
    low = (x - high.astype(F32)).astype(BF16)
    return high, low


def one_hot(index, value):
    rows = lax.broadcasted_iota(jnp.int32, (256, index.shape[1]), 0)
    return jnp.where(rows == (index & 255), value, 0.0).astype(BF16)


def page_table(values_ref, table_ref):
    for h in range(8):
        high, low = halves(values_ref[:, h * 256 : (h + 1) * 256])
        table_ref[h * 64 : h * 64 + 32, :] = high
        table_ref[h * 64 + 32 : h * 64 + 64, :] = low


def page_gather(table_ref, index):
    found = lax.dot_general(table_ref[...], one_hot(index, 1.0), NN, preferred_element_type=F32)
    pages = [found[h * 64 : h * 64 + 32] + found[h * 64 + 32 : h * 64 + 64] for h in range(8)]
    page = jnp.broadcast_to(index >> 8, pages[0].shape)
    picked = pages[0]
    for h in range(1, 8):
        picked = jnp.where(page == h, pages[h], picked)
    return picked


def spread(values, index):
    both = jnp.concatenate(halves(values), axis=0)
    page = index >> 8
    pages = []
    for h in range(8):
        pages.append(both * jnp.where(page == h, 1.0, 0.0).astype(BF16))
    return jnp.concatenate(pages, axis=0)


def page_value(acc_ref, h):
    return acc_ref[h * 64 : h * 64 + 32, :] + acc_ref[h * 64 + 32 : h * 64 + 64, :]


def tile_of(ref, first=0):
    rows = slice(first, first + BCOL)
    return lambda h: ref[rows, h * 128 : (h + 1) * 128]


def apply_inverse(source_ref, perm_ref, inverse_ref, acc_ref, out_ref):
    for chunk in range(4):
        parts = []
        for c in range(4 * chunk, 4 * chunk + 4):
            picked = lane_gather(tile_of(source_ref), 16, perm_ref[0:1, c * 128 : (c + 1) * 128])
            both = jnp.concatenate(halves(picked), axis=0)
            solved = lax.dot_general(both, inverse_ref[c], NN, preferred_element_type=F32)
            parts.append(solved[:BCOL] + solved[BCOL:])
        index = perm_ref[0:1, chunk * 512 : (chunk + 1) * 512]
        part = lax.dot_general(
            spread(jnp.concatenate(parts, axis=1), index),
            one_hot(index, 1.0),
            NT,
            preferred_element_type=F32,
        )
        if chunk == 0:
            acc_ref[...] = part
        else:
            acc_ref[...] += part
    for h in range(8):
        out_ref[:, h * 256 : (h + 1) * 256] = page_value(acc_ref, h)


def fill_sends(values_ref, blocks_ref, count_ref, send_refs, first=0):
    odd = jnp.where(is_odd(), 1, 0)
    rows = slice(first, first + values_ref.shape[0])
    for side, send_ref in zip((1 - odd, odd), send_refs):
        for s in range(8):
            start = pl.multiple_of(blocks_ref[side, s] * 128, 128)
            live = jnp.where(s < count_ref[0, side], 1.0, 0.0)
            send_ref[rows, s * 128 : (s + 1) * 128] = values_ref[:, pl.ds(start, 128)] * live


def start_kernel(
    blocks_hbm, count_hbm, ids_hbm, weight_hbm, rhs_hbm, perm_hbm, inverse_hbm,
    source_ref, smooth_ref, inner_ref, outer_ref,
    acc_ref, blocks_ref, count_ref, ids_ref, weight_ref, perm_ref, inverse_ref, sems,
):
    pairs = (
        (rhs_hbm, source_ref),
        (inverse_hbm, inverse_ref),
        (ids_hbm, ids_ref),
        (weight_hbm, weight_ref),
        (perm_hbm, perm_ref),
        (blocks_hbm, blocks_ref),
        (count_hbm, count_ref),
    )
    copies = [pltpu.make_async_copy(src, dst, sems.at[n]) for n, (src, dst) in enumerate(pairs)]
    for copy in copies:
        copy.start()
    for copy in copies:
        copy.wait()
    first_pore = lax.axis_index("pore") * source_ref.shape[1]
    lanes = lax.broadcasted_iota(jnp.int32, (1, 128), 1)
    for f in range(BCOL):
        place = ids_ref[f] - first_pore
        inside = (place >= 0) & (place < source_ref.shape[1])
        place = jnp.where(inside, place, 0)
        tile = pl.ds(pl.multiple_of((place >> 7) * 128, 128), 128)
        added = jnp.where(inside, weight_ref[f], 0.0)
        source_ref[f : f + 1, tile] += jnp.where(lanes == (place & 127), added, 0.0)
    apply_inverse(source_ref, perm_ref, inverse_ref, acc_ref, smooth_ref)
    fill_sends(smooth_ref, blocks_ref, count_ref, (inner_ref, outer_ref))


def local_kernel(
    values_ref, ends_ref, cond_ref, shift_ref, out_ref, cross_ref, acc_ref, table_ref
):
    block = tile_of(values_ref)
    page_table(values_ref, table_ref)

    def flux_of(part):
        near = page_gather(table_ref, ends_ref[0:1, part])
        far = [
            lane_gather(block, 16, ends_ref[1:2, g : g + 128])
            for g in range(part.start, part.stop, 128)
        ]
        return (near - jnp.concatenate(far, axis=1)) * cond_ref[0:1, part]

    def scattered(flux, part):
        near = ends_ref[0:1, part]
        far = ends_ref[1:2, part]
        left = jnp.concatenate([spread(flux, near), spread(flux, far)], axis=1)
        right = jnp.concatenate([one_hot(near, 1.0), one_hot(far, -1.0)], axis=1)
        return lax.dot_general(left, right, NT, preferred_element_type=F32)

    parts = [slice(start, start + CHUNK) for start in range(0, 4096, CHUNK)]
    flux = flux_of(parts[0])
    for n, part in enumerate(parts):
        later = flux_of(parts[n + 1]) if n + 1 < len(parts) else None
        if n == 0:
            acc_ref[...] = scattered(flux, part)
        else:
            acc_ref[...] += scattered(flux, part)
        flux = later
    for start in range(0, 2048, CHUNK):
        index = ends_ref[0:1, 4096 + start : 4096 + start + CHUNK]
        cross_ref[:, start : start + CHUNK] = page_gather(table_ref, index)
    for h in range(8):
        part = slice(h * 256, (h + 1) * 256)
        out_ref[:, part] = shift_ref[0:1, part] * values_ref[:, part] + page_value(acc_ref, h)


def add_cross(
    partial_ref, cross_ref, inner_ref, outer_ref, ends_ref, cond_ref, acc_ref, face_ref, out_ref
):
    odd = is_odd()
    inner = inner_ref[:BCOL, :]
    outer = outer_ref[:BCOL, :]
    face_ref[0] = jnp.where(odd, inner, outer)
    face_ref[1] = jnp.where(odd, outer, inner)
    for chunk in range(4):
        ref, base = face_ref.at[chunk // 2], 2048 + chunk // 2 * 1024
        drops = []
        for g in range(4 * chunk, 4 * chunk + 4):
            part = slice(4096 + g * 128, 4096 + (g + 1) * 128)
            far = lane_gather(tile_of(ref), 8, ends_ref[1:2, part] - base)
            drops.append(cross_ref[:, g * 128 : (g + 1) * 128] - far)
        part = slice(4096 + chunk * 512, 4096 + (chunk + 1) * 512)
        near = ends_ref[0:1, part]
        flux = jnp.concatenate(drops, axis=1) * cond_ref[0:1, part]
        product = lax.dot_general(
            spread(flux, near), one_hot(near, 1.0), NT, preferred_element_type=F32
        )
        if chunk == 0:
            acc_ref[...] = product
        else:
            acc_ref[...] += product
    for h in range(8):
        part = slice(h * 256, (h + 1) * 256)
        out_ref[:, part] = partial_ref[:, part] + page_value(acc_ref, h)


def step_kernel(
    blocks_ref, count_ref, partial_ref, cross_ref, inner_ref, outer_ref, ends_ref, cond_ref,
    perm_ref, inverse_ref, mapped_ref, smooth_ref, inner_send, outer_send, acc_ref, face_ref,
):
    add_cross(
        partial_ref, cross_ref, inner_ref, outer_ref, ends_ref, cond_ref, acc_ref, face_ref, mapped_ref
    )
    apply_inverse(mapped_ref, perm_ref, inverse_ref, acc_ref, smooth_ref)
    fill_sends(smooth_ref, blocks_ref, count_ref, (inner_send, outer_send))


def first_step_kernel(blocks_ref, count_ref, pressure_ref, *refs):
    step_kernel(blocks_ref, count_ref, *refs)
    sends = refs[10:12]
    for ref in sends:
        ref[BCOL:, :] = jnp.zeros((8, 1024), F32)
    fill_sends(pressure_ref, blocks_ref, count_ref, sends, BCOL)


def exact_dot(a, b, dims):
    return lax.dot_general(a, b, dims, precision=lax.Precision.HIGHEST, preferred_element_type=F32)


def square_index():
    return (lax.broadcasted_iota(jnp.int32, (BCOL, BCOL), axis) for axis in (0, 1))


def packed(moments):
    row, column = square_index()
    pairs, diagonals = [], []
    for upper, lower in zip(moments[::2], moments[1::2]):
        pairs.append(jnp.where(row <= column, upper, lower))
        diagonals.append(jnp.sum(jnp.where(row == column, lower, 0.0), axis=0, keepdims=True))
    diagonals.append(jnp.zeros((BCOL - 3, BCOL), F32))
    return jnp.concatenate(pairs + [jnp.concatenate(diagonals, axis=0)], axis=1)


def unpacked(table):
    row, column = square_index()
    turned = table.T
    moments = []
    for n in range(3):
        pair = table[:, BCOL * n : BCOL * (n + 1)]
        mirror = turned[BCOL * n : BCOL * (n + 1), :]
        diagonal = table[n : n + 1, 3 * BCOL :]
        moments.append(jnp.where(row <= column, pair, mirror))
        outside = jnp.where(row > column, pair, mirror)
        moments.append(jnp.where(row == column, diagonal, outside))
    return moments


def last_kernel(
    partial_ref, cross_ref, inner_ref, outer_ref, ends_ref, cond_ref,
    z0_ref, z1_ref, z2_ref, q0_ref, q1_ref, source_ref, mapped_ref, moment_ref, acc_ref, face_ref,
):
    add_cross(
        partial_ref, cross_ref, inner_ref, outer_ref, ends_ref, cond_ref, acc_ref, face_ref, mapped_ref
    )
    smooth = jnp.concatenate([z0_ref[...], z1_ref[...], z2_ref[...]], axis=0)
    mapped = jnp.concatenate([q0_ref[...], q1_ref[...], mapped_ref[...], source_ref[...]], axis=0)
    products = lax.dot_general(
        jnp.concatenate(halves(smooth), axis=0),
        jnp.concatenate(halves(mapped), axis=0),
        NT,
        preferred_element_type=F32,
    )
    gram = products[:96] + products[96:]
    gram = gram[:, :128] + gram[:, 128:]
    z0, z1, z2 = gram[:32], gram[32:64], gram[64:]
    moments = packed(
        (z0[:, 96:], z0[:, :32], z1[:, :32], z1[:, 32:64], z2[:, 32:64], z2[:, 64:96])
    )
    for n in range(moment_ref.shape[0]):
        moment_ref[n] = moments


def solved_table(table):
    tiles = [table[8 * v : 8 * v + 8, :] for v in range(12)]
    row_at = lax.broadcasted_iota(jnp.int32, (8, 128), 0)
    for first in range(0, 96, SIDE):
        columns = [
            [jnp.broadcast_to(tile[:, first + p : first + p + 1], (8, 128)) for p in range(SIDE)]
            for tile in tiles
        ]
        own = range(first // 8, (first + SIDE) // 8)
        pivots = {u: list(columns[u]) for u in own}
        solved = {u: tiles[u] for u in own}
        for p in range(SIDE):
            v, r = divmod(first + p, 8)
            inverse = 1.0 / pivots[v][p][r : r + 1, :]
            row = solved[v][r : r + 1, :] * inverse
            factors = [pivots[v][q][r : r + 1, :] * inverse for q in range(p + 1, SIDE)]
            for u in own:
                solved[u] = solved[u] - pivots[u][p] * row
                for q, factor in zip(range(p + 1, SIDE), factors):
                    pivots[u][q] = pivots[u][q] - pivots[u][p] * factor
            solved[v] = jnp.where(row_at == r, row, solved[v])
            for q, factor in zip(range(p + 1, SIDE), factors):
                pivots[v][q] = jnp.where(row_at == r, factor, pivots[v][q])
        for u in range(12):
            if u in own:
                tiles[u] = solved[u]
                continue
            products = [
                columns[u][p] * solved[(first + p) // 8][p % 8 : p % 8 + 1, :] for p in range(SIDE)
            ]
            while len(products) > 1:
                products = [a + b for a, b in zip(products[::2], products[1::2])]
            tiles[u] = tiles[u] - products[0]
    return tiles


def ends_tile(ends_ref, end, v):
    rows = [ends_ref[end : end + 1, j * 128 : (j + 1) * 128] for j in range(8 * v, 8 * v + 8)]
    return jnp.concatenate(rows, axis=0)


def throat_drop(row_ref, ends_ref, v):
    def block_at(offset):
        return lambda h: row_ref[:, offset + h * 128 : offset + (h + 1) * 128]

    offset, blocks = ((0, 16), (2048, 8), (3072, 8))[max(v - 3, 0)]
    near = lane_gather(block_at(0), 16, ends_tile(ends_ref, 0, v))
    return near - lane_gather(block_at(offset), blocks, ends_tile(ends_ref, 1, v) - offset)


def place_faces(row_ref, inner, outer):
    odd = is_odd()
    row_ref[:, 2048:3072] = jnp.broadcast_to(jnp.where(odd, inner, outer), (8, 1024))
    row_ref[:, 3072:4096] = jnp.broadcast_to(jnp.where(odd, outer, inner), (8, 1024))


def pressure_kernel(pressure_ref, inner_ref, outer_ref, ends_ref, drop_ref, row_ref):
    row_ref[:, 0:2048] = jnp.broadcast_to(pressure_ref[0:1, :], (8, 2048))
    place_faces(row_ref, inner_ref[BCOL : BCOL + 1, :], outer_ref[BCOL : BCOL + 1, :])
    for v in range(6):
        drop = throat_drop(row_ref, ends_ref, v)
        drop_ref[8 * v : 8 * v + 8, :] = drop * (-1.0 / math.sqrt(FIELDS))


def solve_kernel(
    mine_ref, other_ref, z0_ref, z1_ref, z2_ref, i0_ref, i1_ref, i2_ref, o0_ref, o1_ref, o2_ref,
    drop_ref, ends_ref, coeff_ref, term_ref, row_ref, total_ref,
):
    m = unpacked(mine_ref[...] + other_ref[...])
    rows = [jnp.concatenate([m[n + 1], m[n + 2], m[n + 3], m[n]], axis=1) for n in range(3)]
    tiles = solved_table(jnp.concatenate(rows, axis=0))
    for v in range(12):
        coeff_ref[8 * v : 8 * v + 8, :] = tiles[v][:, 96:]
    weights = [
        jnp.broadcast_to(jnp.sum(tile[:, 96:], axis=1, keepdims=True), (8, 128)) for tile in tiles
    ]

    def weighted(refs, start):
        part = slice(start, start + 128)
        total = None
        for v in range(12):
            ref = refs[v // 4]
            product = weights[v] * ref[8 * (v % 4) : 8 * (v % 4) + 8, part]
            total = product if total is None else total + product
        return jnp.sum(total, axis=0, keepdims=True)

    for start in range(0, 2048, 128):
        row_ref[:, start : start + 128] = jnp.broadcast_to(
            weighted((z0_ref, z1_ref, z2_ref), start), (8, 128)
        )
    inner, outer = (
        jnp.concatenate([weighted(refs, start) for start in range(0, 1024, 128)], axis=1)
        for refs in ((i0_ref, i1_ref, i2_ref), (o0_ref, o1_ref, o2_ref))
    )
    place_faces(row_ref, inner, outer)
    for v in range(6):
        drop = throat_drop(row_ref, ends_ref, v)
        total_ref[8 * v : 8 * v + 8, :] = drop * drop_ref[8 * v : 8 * v + 8, :]
    for n in range(8):
        term_ref[n] = total_ref[6 * n : 6 * n + 6, :]


def finish_kernel(
    coeff_ref, z0_ref, z1_ref, z2_ref, q0_ref, q1_ref, q2_ref, source_ref, adjoint_ref, residual_ref
):
    coeff = coeff_ref[...]
    smooth = jnp.concatenate([z0_ref[...], z1_ref[...], z2_ref[...]], axis=0)
    mapped = jnp.concatenate([q0_ref[...], q1_ref[...], q2_ref[...]], axis=0)
    adjoint_ref[...] = exact_dot(coeff, smooth, TN)
    residual_ref[...] = source_ref[...] - exact_dot(coeff, mapped, TN)


def call(kernel, spaces, args, outs, scratch, name, flops=0, limit=32 << 10):
    return pl.pallas_call(
        kernel,
        out_shape=[jax.ShapeDtypeStruct(s, F32) for s in outs],
        in_specs=[pl.BlockSpec(memory_space=space) for space in spaces],
        out_specs=[pl.BlockSpec(memory_space=pltpu.VMEM)] * len(outs),
        scratch_shapes=scratch,
        compiler_params=pltpu.CompilerParams(vmem_limit_bytes=limit << 10),
        cost_estimate=pl.CostEstimate(flops=flops, bytes_accessed=2 << 20, transcendentals=0),
        name=name,
    )(*args)


def shards(
    rhs, well_ids, well_weight, pressure, shift, conductance, throat_ends, boundary_blocks,
    boundary_count, jacobi_perm, jacobi_inverse,
):
    pores = rhs.shape[1]
    perm = jacobi_perm[None, :]
    pressure_row = pressure[None, :]
    shift_row = shift[None, :]
    cond = conductance[None, :]
    field = (BCOL, pores)
    sent = (BCOL, 1024)
    smem, vmem = pltpu.SMEM, pltpu.VMEM
    acc = pltpu.VMEM((512, 256), F32)
    table = pltpu.VMEM((512, 256), BF16)
    face = pltpu.VMEM((2, *sent), F32)
    work = 12 * 10**9

    counts = boundary_count.T
    chips = lax.axis_size("pore") // 2
    source, z, *sends = call(
        start_kernel, [pltpu.HBM] * 7,
        (boundary_blocks, counts, well_ids, well_weight, rhs, perm, jacobi_inverse),
        (field, field, sent, sent),
        [
            acc, smem(boundary_blocks.shape, jnp.int32), smem(counts.shape, jnp.int32),
            smem(well_ids.shape, jnp.int32), smem(well_weight.shape, F32),
            vmem(perm.shape, jnp.int32), vmem(jacobi_inverse.shape, BF16),
            pltpu.SemaphoreType.DMA((7,)),
        ],
        "start", limit=53 << 10,
    )
    smooths, mappeds, inners, outers = [], [], [], []
    for k in range(ITERS):
        inner, outer = swapped_faces(*sends)
        partial, cross = call(
            local_kernel, [vmem] * 4, (z, throat_ends, cond, shift_row),
            (field, field), [acc, table], "local", work,
        )
        smooths.append(z)
        inners.append(inner)
        outers.append(outer)
        met = (partial, cross, inner, outer, throat_ends, cond)
        if k + 1 < ITERS:
            extra = (pressure_row,) if k == 0 else ()
            faces = (BCOL + 8 * len(extra), 1024)
            mapped, z, *sends = call(
                step_kernel if k else first_step_kernel, [smem] * 2 + [vmem] * (8 + len(extra)),
                (boundary_blocks, counts, *extra, *met, perm, jacobi_inverse),
                (field, field, faces, faces), [acc, face], "step",
            )
        else:
            mapped, moments = call(
                last_kernel, [vmem] * 12, met + (*smooths, *mappeds, source),
                (field, (chips, BCOL, 128)), [acc, face], "last",
            )
        mappeds.append(mapped)
    mine, other = pore_sum(moments)
    row = pltpu.VMEM((8, 4096), F32)
    (drop,) = call(
        pressure_kernel, [vmem] * 4, (pressure_row, inners[1], outers[1], throat_ends),
        ((48, 128),), [row], "pressure", work,
    )
    coeff, term = call(
        solve_kernel, [vmem] * 13, (mine, other, *smooths, *inners, *outers, drop, throat_ends),
        ((96, BCOL), (8, 6, 128)), [row, pltpu.VMEM((48, 128), F32)], "solve",
    )
    shared = lax.all_to_all(term, "field", 0, 0, tiled=True)
    adjoint, residual = call(
        finish_kernel, [vmem] * 8, (coeff, *smooths, *mappeds, source), (field, field), [],
        "finish", work,
    )
    gradient = jnp.sum(shared, axis=0).reshape(-1)
    return (adjoint, residual, gradient)


def solution(mesh):
    in_specs = (
        P("field", "pore"),
        P("field"),
        P("field"),
        P("pore"),
        P("pore"),
        P("pore"),
        P(None, "pore"),
        P(None, "pore"),
        P(None, "pore"),
        P("pore"),
        P("pore", None, None),
    )
    out_specs = (P("field", "pore"), P("field", "pore"), P(("pore", "field")))
    return jax.shard_map(shards, mesh=mesh, in_specs=in_specs, out_specs=out_specs, check_vma=False)
```

```python
import functools
import math

import jax
import jax.numpy as jnp
from jax import lax
from jax.experimental import pallas as pl
from jax.experimental.pallas import tpu as pltpu
from jax.sharding import PartitionSpec as P

FIELDS = 256
BCOL = 32
ITERS = 3
NT = (((1,), (1,)), ((), ()))
NN = (((1,), (0,)), ((), ()))
TN = (((0,), (0,)), ((), ()))
F32 = jnp.float32
BF16 = jnp.bfloat16
CHUNK = 512
SIDE = 16


def permuted(x, axis, target):
    devices = lax.axis_size(axis)
    pairs = [(i, target(i)) for i in range(devices) if 0 <= target(i) < devices]
    return lax.ppermute(x, axis, pairs)


def pore_sum(copies):
    chips = copies.shape[0]
    groups = [[2 * chip + core for chip in range(chips)] for core in range(2)]
    received = lax.all_to_all(copies, "pore", 0, 0, axis_index_groups=groups, tiled=True)
    mine = jnp.sum(received, axis=0)
    return mine, permuted(mine, "pore", lambda i: i ^ 1)


def swapped_faces(even_face, odd_face):
    inner = permuted(even_face, "pore", lambda i: i ^ 1)
    devices = lax.axis_size("pore")
    outer = permuted(odd_face, "pore", lambda i: (((i + 1) % devices ^ 1) - 1) % devices)
    return inner, outer


def is_odd():
    return lax.axis_index("pore") % 2 == 1


def lane_gather(block, blocks, index):
    shape = block(0).shape
    low = jnp.broadcast_to(index & 127, shape)
    high = jnp.broadcast_to(index >> 7, shape)
    found = jnp.take_along_axis(block(0), low, axis=1)
    for h in range(1, blocks):
        found = jnp.where(high == h, jnp.take_along_axis(block(h), low, axis=1), found)
    return found


def halves(x):
    high = x.astype(BF16)
    low = (x - high.astype(F32)).astype(BF16)
    return high, low


def one_hot(index, value):
    rows = lax.broadcasted_iota(jnp.int32, (256, index.shape[1]), 0)
    return jnp.where(rows == (index & 255), value, 0.0).astype(BF16)


def page_table(values_ref, table_ref):
    for h in range(8):
        high, low = halves(values_ref[:, h * 256 : (h + 1) * 256])
        table_ref[h * 64 : h * 64 + 32, :] = high
        table_ref[h * 64 + 32 : h * 64 + 64, :] = low


def page_gather(table_ref, index):
    found = lax.dot_general(table_ref[...], one_hot(index, 1.0), NN, preferred_element_type=F32)
    pages = [found[h * 64 : h * 64 + 32] + found[h * 64 + 32 : h * 64 + 64] for h in range(8)]
    page = jnp.broadcast_to(index >> 8, pages[0].shape)
    picked = pages[0]
    for h in range(1, 8):
        picked = jnp.where(page == h, pages[h], picked)
    return picked


def spread(values, index):
    both = jnp.concatenate(halves(values), axis=0)
    page = index >> 8
    pages = []
    for h in range(8):
        pages.append(both * jnp.where(page == h, 1.0, 0.0).astype(BF16))
    return jnp.concatenate(pages, axis=0)


def page_value(acc_ref, h):
    return acc_ref[h * 64 : h * 64 + 32, :] + acc_ref[h * 64 + 32 : h * 64 + 64, :]


def tile_of(ref, first=0):
    rows = slice(first, first + BCOL)
    return lambda h: ref[rows, h * 128 : (h + 1) * 128]


def apply_inverse(source_ref, perm_ref, inverse_ref, acc_ref, out_ref):
    for chunk in range(4):
        parts = []
        for c in range(4 * chunk, 4 * chunk + 4):
            picked = lane_gather(tile_of(source_ref), 16, perm_ref[0:1, c * 128 : (c + 1) * 128])
            both = jnp.concatenate(halves(picked), axis=0)
            solved = lax.dot_general(both, inverse_ref[c], NN, preferred_element_type=F32)
            parts.append(solved[:BCOL] + solved[BCOL:])
        index = perm_ref[0:1, chunk * 512 : (chunk + 1) * 512]
        part = lax.dot_general(
            spread(jnp.concatenate(parts, axis=1), index),
            one_hot(index, 1.0),
            NT,
            preferred_element_type=F32,
        )
        if chunk == 0:
            acc_ref[...] = part
        else:
            acc_ref[...] += part
    for h in range(8):
        out_ref[:, h * 256 : (h + 1) * 256] = page_value(acc_ref, h)


def fill_sends(values_ref, blocks_ref, count_ref, send_refs, first=0):
    odd = jnp.where(is_odd(), 1, 0)
    rows = slice(first, first + values_ref.shape[0])
    place = lax.axis_index("pore")
    met = (place > 0) & (place < lax.axis_size("pore") - 1)
    for side, faced, send_ref in zip((1 - odd, odd), (True, met), send_refs):
        count = jnp.where(faced, count_ref[0, side], 0)
        for s in range(8):
            start = pl.multiple_of(blocks_ref[side, s] * 128, 128)
            live = jnp.where(s < count, 1.0, 0.0)
            send_ref[rows, s * 128 : (s + 1) * 128] = values_ref[:, pl.ds(start, 128)] * live


def start_kernel(
    blocks_hbm, count_hbm, ids_hbm, weight_hbm, rhs_hbm, perm_hbm, inverse_hbm,
    source_ref, smooth_ref, inner_ref, outer_ref,
    acc_ref, blocks_ref, count_ref, ids_ref, weight_ref, perm_ref, inverse_ref, sems,
):
    pairs = (
        (rhs_hbm, source_ref),
        (inverse_hbm, inverse_ref),
        (ids_hbm, ids_ref),
        (weight_hbm, weight_ref),
        (perm_hbm, perm_ref),
        (blocks_hbm, blocks_ref),
        (count_hbm, count_ref),
    )
    copies = [pltpu.make_async_copy(src, dst, sems.at[n]) for n, (src, dst) in enumerate(pairs)]
    for copy in copies:
        copy.start()
    for n, copy in enumerate(copies):
        if n != 1:
            copy.wait()
    first_pore = lax.axis_index("pore") * source_ref.shape[1]
    lanes = lax.broadcasted_iota(jnp.int32, (1, 128), 1)
    for f in range(BCOL):
        place = ids_ref[f] - first_pore
        inside = (place >= 0) & (place < source_ref.shape[1])
        place = jnp.where(inside, place, 0)
        tile = pl.ds(pl.multiple_of((place >> 7) * 128, 128), 128)
        added = jnp.where(inside, weight_ref[f], 0.0)
        source_ref[f : f + 1, tile] += jnp.where(lanes == (place & 127), added, 0.0)
    copies[1].wait()
    apply_inverse(source_ref, perm_ref, inverse_ref, acc_ref, smooth_ref)
    fill_sends(smooth_ref, blocks_ref, count_ref, (inner_ref, outer_ref))


def local_kernel(
    values_ref, ends_ref, cond_ref, shift_ref, out_ref, cross_ref, acc_ref, table_ref
):
    block = tile_of(values_ref)
    page_table(values_ref, table_ref)

    def flux_of(part):
        near = page_gather(table_ref, ends_ref[0:1, part])
        far = [
            lane_gather(block, 16, ends_ref[1:2, g : g + 128])
            for g in range(part.start, part.stop, 128)
        ]
        return (near - jnp.concatenate(far, axis=1)) * cond_ref[0:1, part]

    def scattered(flux, part):
        near = ends_ref[0:1, part]
        far = ends_ref[1:2, part]
        left = jnp.concatenate([spread(flux, near), spread(flux, far)], axis=1)
        right = jnp.concatenate([one_hot(near, 1.0), one_hot(far, -1.0)], axis=1)
        return lax.dot_general(left, right, NT, preferred_element_type=F32)

    parts = [slice(start, start + CHUNK) for start in range(0, 4096, CHUNK)]
    flux = flux_of(parts[0])
    for n, part in enumerate(parts):
        later = flux_of(parts[n + 1]) if n + 1 < len(parts) else None
        if n == 0:
            acc_ref[...] = scattered(flux, part)
        else:
            acc_ref[...] += scattered(flux, part)
        flux = later
    for start in range(0, 2048, CHUNK):
        index = ends_ref[0:1, 4096 + start : 4096 + start + CHUNK]
        cross_ref[:, start : start + CHUNK] = page_gather(table_ref, index)
    for h in range(8):
        part = slice(h * 256, (h + 1) * 256)
        out_ref[:, part] = shift_ref[0:1, part] * values_ref[:, part] + page_value(acc_ref, h)


def add_cross(
    partial_ref, cross_ref, inner_ref, outer_ref, ends_ref, cond_ref, acc_ref, face_ref, out_ref
):
    odd = is_odd()
    inner = inner_ref[:BCOL, :]
    outer = outer_ref[:BCOL, :]
    face_ref[0] = jnp.where(odd, inner, outer)
    face_ref[1] = jnp.where(odd, outer, inner)
    for chunk in range(4):
        ref, base = face_ref.at[chunk // 2], 2048 + chunk // 2 * 1024
        drops = []
        for g in range(4 * chunk, 4 * chunk + 4):
            part = slice(4096 + g * 128, 4096 + (g + 1) * 128)
            far = lane_gather(tile_of(ref), 8, ends_ref[1:2, part] - base)
            drops.append(cross_ref[:, g * 128 : (g + 1) * 128] - far)
        part = slice(4096 + chunk * 512, 4096 + (chunk + 1) * 512)
        near = ends_ref[0:1, part]
        flux = jnp.concatenate(drops, axis=1) * cond_ref[0:1, part]
        product = lax.dot_general(
            spread(flux, near), one_hot(near, 1.0), NT, preferred_element_type=F32
        )
        if chunk == 0:
            acc_ref[...] = product
        else:
            acc_ref[...] += product
    for h in range(8):
        part = slice(h * 256, (h + 1) * 256)
        out_ref[:, part] = partial_ref[:, part] + page_value(acc_ref, h)


def step_kernel(
    blocks_ref, count_ref, partial_ref, cross_ref, inner_ref, outer_ref, ends_ref, cond_ref,
    perm_ref, inverse_ref, mapped_ref, smooth_ref, inner_send, outer_send, acc_ref, face_ref,
):
    add_cross(
        partial_ref, cross_ref, inner_ref, outer_ref, ends_ref, cond_ref, acc_ref, face_ref, mapped_ref
    )
    apply_inverse(mapped_ref, perm_ref, inverse_ref, acc_ref, smooth_ref)
    fill_sends(smooth_ref, blocks_ref, count_ref, (inner_send, outer_send))


def first_step_kernel(blocks_ref, count_ref, pressure_ref, *refs):
    step_kernel(blocks_ref, count_ref, *refs)
    sends = refs[10:12]
    for ref in sends:
        ref[BCOL:, :] = jnp.zeros((8, 1024), F32)
    fill_sends(pressure_ref, blocks_ref, count_ref, sends, BCOL)


def exact_dot(a, b, dims):
    return lax.dot_general(a, b, dims, precision=lax.Precision.HIGHEST, preferred_element_type=F32)


def square_index():
    return (lax.broadcasted_iota(jnp.int32, (BCOL, BCOL), axis) for axis in (0, 1))


def packed(moments):
    row, column = square_index()
    pairs, diagonals = [], []
    for upper, lower in zip(moments[::2], moments[1::2]):
        pairs.append(jnp.where(row <= column, upper, lower))
        diagonals.append(jnp.sum(jnp.where(row == column, lower, 0.0), axis=0, keepdims=True))
    diagonals.append(jnp.zeros((BCOL - 3, BCOL), F32))
    return jnp.concatenate(pairs + [jnp.concatenate(diagonals, axis=0)], axis=1)


def unpacked(table):
    row, column = square_index()
    turned = table.T
    moments = []
    for n in range(3):
        pair = table[:, BCOL * n : BCOL * (n + 1)]
        mirror = turned[BCOL * n : BCOL * (n + 1), :]
        diagonal = table[n : n + 1, 3 * BCOL :]
        moments.append(jnp.where(row <= column, pair, mirror))
        outside = jnp.where(row > column, pair, mirror)
        moments.append(jnp.where(row == column, diagonal, outside))
    return moments


def last_kernel(
    partial_ref, cross_ref, inner_ref, outer_ref, ends_ref, cond_ref,
    z0_ref, z1_ref, z2_ref, q0_ref, q1_ref, source_ref, mapped_ref, moment_ref, acc_ref, face_ref,
):
    add_cross(
        partial_ref, cross_ref, inner_ref, outer_ref, ends_ref, cond_ref, acc_ref, face_ref, mapped_ref
    )
    smooth = jnp.concatenate([z0_ref[...], z1_ref[...], z2_ref[...]], axis=0)
    mapped = jnp.concatenate([q0_ref[...], q1_ref[...], mapped_ref[...], source_ref[...]], axis=0)
    products = lax.dot_general(
        jnp.concatenate(halves(smooth), axis=0),
        jnp.concatenate(halves(mapped), axis=0),
        NT,
        preferred_element_type=F32,
    )
    gram = products[:96] + products[96:]
    gram = gram[:, :128] + gram[:, 128:]
    z0, z1, z2 = gram[:32], gram[32:64], gram[64:]
    moments = packed(
        (z0[:, 96:], z0[:, :32], z1[:, :32], z1[:, 32:64], z2[:, 32:64], z2[:, 64:96])
    )
    for n in range(moment_ref.shape[0]):
        moment_ref[n] = moments


def solved_table(table):
    tiles = [table[8 * v : 8 * v + 8, :] for v in range(12)]
    row_at = lax.broadcasted_iota(jnp.int32, (8, 128), 0)
    for first in range(0, 96, SIDE):
        columns = [
            [jnp.broadcast_to(tile[:, first + p : first + p + 1], (8, 128)) for p in range(SIDE)]
            for tile in tiles
        ]
        own = range(first // 8, (first + SIDE) // 8)
        pivots = {u: list(columns[u]) for u in own}
        solved = {u: tiles[u] for u in own}
        for p in range(SIDE):
            v, r = divmod(first + p, 8)
            inverse = 1.0 / pivots[v][p][r : r + 1, :]
            row = solved[v][r : r + 1, :] * inverse
            factors = [pivots[v][q][r : r + 1, :] * inverse for q in range(p + 1, SIDE)]
            for u in own:
                solved[u] = solved[u] - pivots[u][p] * row
                for q, factor in zip(range(p + 1, SIDE), factors):
                    pivots[u][q] = pivots[u][q] - pivots[u][p] * factor
            solved[v] = jnp.where(row_at == r, row, solved[v])
            for q, factor in zip(range(p + 1, SIDE), factors):
                pivots[v][q] = jnp.where(row_at == r, factor, pivots[v][q])
        for u in range(12):
            if u in own:
                tiles[u] = solved[u]
                continue
            products = [
                columns[u][p] * solved[(first + p) // 8][p % 8 : p % 8 + 1, :] for p in range(SIDE)
            ]
            while len(products) > 1:
                products = [a + b for a, b in zip(products[::2], products[1::2])]
            tiles[u] = tiles[u] - products[0]
    return tiles


def ends_tile(ends_ref, end, v):
    rows = [ends_ref[end : end + 1, j * 128 : (j + 1) * 128] for j in range(8 * v, 8 * v + 8)]
    return jnp.concatenate(rows, axis=0)


def throat_drop(row_ref, ends_ref, v):
    def block_at(offset):
        return lambda h: row_ref[:, offset + h * 128 : offset + (h + 1) * 128]

    offset, blocks = ((0, 16), (2048, 8), (3072, 8))[max(v - 3, 0)]
    near = lane_gather(block_at(0), 16, ends_tile(ends_ref, 0, v))
    return near - lane_gather(block_at(offset), blocks, ends_tile(ends_ref, 1, v) - offset)


def place_faces(row_ref, inner, outer):
    odd = is_odd()
    row_ref[:, 2048:3072] = jnp.broadcast_to(jnp.where(odd, inner, outer), (8, 1024))
    row_ref[:, 3072:4096] = jnp.broadcast_to(jnp.where(odd, outer, inner), (8, 1024))


def pressure_kernel(pressure_ref, inner_ref, outer_ref, ends_ref, drop_ref, row_ref):
    row_ref[:, 0:2048] = jnp.broadcast_to(pressure_ref[0:1, :], (8, 2048))
    place_faces(row_ref, inner_ref[BCOL : BCOL + 1, :], outer_ref[BCOL : BCOL + 1, :])
    for v in range(6):
        drop = throat_drop(row_ref, ends_ref, v)
        drop_ref[8 * v : 8 * v + 8, :] = drop * (-1.0 / math.sqrt(FIELDS))


def solve_kernel(
    mine_ref, other_ref, z0_ref, z1_ref, z2_ref, i0_ref, i1_ref, i2_ref, o0_ref, o1_ref, o2_ref,
    drop_ref, ends_ref, coeff_ref, term_ref, row_ref, total_ref,
):
    m = unpacked(mine_ref[...] + other_ref[...])
    rows = [jnp.concatenate([m[n + 1], m[n + 2], m[n + 3], m[n]], axis=1) for n in range(3)]
    tiles = solved_table(jnp.concatenate(rows, axis=0))
    for v in range(12):
        coeff_ref[8 * v : 8 * v + 8, :] = tiles[v][:, 96:]
    weights = [
        jnp.broadcast_to(jnp.sum(tile[:, 96:], axis=1, keepdims=True), (8, 128)) for tile in tiles
    ]

    def weighted(refs, start):
        part = slice(start, start + 128)
        total = None
        for v in range(12):
            ref = refs[v // 4]
            product = weights[v] * ref[8 * (v % 4) : 8 * (v % 4) + 8, part]
            total = product if total is None else total + product
        return jnp.sum(total, axis=0, keepdims=True)

    for start in range(0, 2048, 128):
        row_ref[:, start : start + 128] = jnp.broadcast_to(
            weighted((z0_ref, z1_ref, z2_ref), start), (8, 128)
        )
    inner, outer = (
        jnp.concatenate([weighted(refs, start) for start in range(0, 1024, 128)], axis=1)
        for refs in ((i0_ref, i1_ref, i2_ref), (o0_ref, o1_ref, o2_ref))
    )
    place_faces(row_ref, inner, outer)
    for v in range(6):
        drop = throat_drop(row_ref, ends_ref, v)
        total_ref[8 * v : 8 * v + 8, :] = drop * drop_ref[8 * v : 8 * v + 8, :]
    for n in range(8):
        term_ref[n] = total_ref[6 * n : 6 * n + 6, :]


def finish_kernel(
    coeff_ref, z0_ref, z1_ref, z2_ref, q0_ref, q1_ref, q2_ref, source_ref, adjoint_ref, residual_ref
):
    coeff = coeff_ref[...]
    smooth = jnp.concatenate([z0_ref[...], z1_ref[...], z2_ref[...]], axis=0)
    mapped = jnp.concatenate([q0_ref[...], q1_ref[...], q2_ref[...]], axis=0)
    adjoint_ref[...] = exact_dot(coeff, smooth, TN)
    residual_ref[...] = source_ref[...] - exact_dot(coeff, mapped, TN)


def call(kernel, spaces, args, outs, scratch, name, flops=0, limit=32 << 10):
    return pl.pallas_call(
        kernel,
        out_shape=[jax.ShapeDtypeStruct(s, F32) for s in outs],
        in_specs=[pl.BlockSpec(memory_space=space) for space in spaces],
        out_specs=[pl.BlockSpec(memory_space=pltpu.VMEM)] * len(outs),
        scratch_shapes=scratch,
        compiler_params=pltpu.CompilerParams(vmem_limit_bytes=limit << 10),
        cost_estimate=pl.CostEstimate(flops=flops, bytes_accessed=2 << 20, transcendentals=0),
        name=name,
    )(*args)


def shards(
    rhs, well_ids, well_weight, pressure, shift, conductance, throat_ends, boundary_blocks,
    boundary_count, jacobi_perm, jacobi_inverse,
):
    pores = rhs.shape[1]
    perm = jacobi_perm[None, :]
    pressure_row = pressure[None, :]
    shift_row = shift[None, :]
    cond = conductance[None, :]
    field = (BCOL, pores)
    sent = (BCOL, 1024)
    smem, vmem = pltpu.SMEM, pltpu.VMEM
    acc = pltpu.VMEM((512, 256), F32)
    table = pltpu.VMEM((512, 256), BF16)
    face = pltpu.VMEM((2, *sent), F32)
    work = 12 * 10**9

    counts = boundary_count.T
    chips = lax.axis_size("pore") // 2
    source, z, *sends = call(
        start_kernel, [pltpu.HBM] * 7,
        (boundary_blocks, counts, well_ids, well_weight, rhs, perm, jacobi_inverse),
        (field, field, sent, sent),
        [
            acc, smem(boundary_blocks.shape, jnp.int32), smem(counts.shape, jnp.int32),
            smem(well_ids.shape, jnp.int32), smem(well_weight.shape, F32),
            vmem(perm.shape, jnp.int32), vmem(jacobi_inverse.shape, BF16),
            pltpu.SemaphoreType.DMA((7,)),
        ],
        "start", limit=53 << 10,
    )
    smooths, mappeds, inners, outers = [], [], [], []
    for k in range(ITERS):
        inner, outer = swapped_faces(*sends)
        partial, cross = call(
            local_kernel, [vmem] * 4, (z, throat_ends, cond, shift_row),
            (field, field), [acc, table], "local", work,
        )
        smooths.append(z)
        inners.append(inner)
        outers.append(outer)
        met = (partial, cross, inner, outer, throat_ends, cond)
        if k + 1 < ITERS:
            extra = (pressure_row,) if k == 0 else ()
            faces = (BCOL + 8 * len(extra), 1024)
            mapped, z, *sends = call(
                step_kernel if k else first_step_kernel, [smem] * 2 + [vmem] * (8 + len(extra)),
                (boundary_blocks, counts, *extra, *met, perm, jacobi_inverse),
                (field, field, faces, faces), [acc, face], "step",
            )
        else:
            mapped, moments = call(
                last_kernel, [vmem] * 12, met + (*smooths, *mappeds, source),
                (field, (chips, BCOL, 128)), [acc, face], "last",
            )
        mappeds.append(mapped)
    mine, other = pore_sum(moments)
    row = pltpu.VMEM((8, 4096), F32)
    (drop,) = call(
        pressure_kernel, [vmem] * 4, (pressure_row, inners[1], outers[1], throat_ends),
        ((48, 128),), [row], "pressure", work,
    )
    coeff, term = call(
        solve_kernel, [vmem] * 13, (mine, other, *smooths, *inners, *outers, drop, throat_ends),
        ((96, BCOL), (8, 6, 128)), [row, pltpu.VMEM((48, 128), F32)], "solve",
    )
    shared = lax.all_to_all(term, "field", 0, 0, tiled=True)
    adjoint, residual = call(
        finish_kernel, [vmem] * 8, (coeff, *smooths, *mappeds, source), (field, field), [],
        "finish", work,
    )
    gradient = jnp.sum(shared, axis=0).reshape(-1)
    return (adjoint, residual, gradient)


def solution(mesh):
    in_specs = (
        P("field", "pore"),
        P("field"),
        P("field"),
        P("pore"),
        P("pore"),
        P("pore"),
        P(None, "pore"),
        P(None, "pore"),
        P(None, "pore"),
        P("pore"),
        P("pore", None, None),
    )
    out_specs = (P("field", "pore"), P("field", "pore"), P(("pore", "field")))
    return jax.shard_map(shards, mesh=mesh, in_specs=in_specs, out_specs=out_specs, check_vma=False)
```

```python
import functools
import math

import jax
import jax.numpy as jnp
from jax import lax
from jax.experimental import pallas as pl
from jax.experimental.pallas import tpu as pltpu
from jax.sharding import PartitionSpec as P

FIELDS = 256
BCOL = 32
ITERS = 3
NT = (((1,), (1,)), ((), ()))
NN = (((1,), (0,)), ((), ()))
TN = (((0,), (0,)), ((), ()))
F32 = jnp.float32
BF16 = jnp.bfloat16
CHUNK = 512
SIDE = 16


def permuted(x, axis, target):
    devices = lax.axis_size(axis)
    pairs = [(i, target(i)) for i in range(devices) if 0 <= target(i) < devices]
    return lax.ppermute(x, axis, pairs)


def pore_sum(copies):
    chips = copies.shape[0]
    groups = [[2 * chip + core for chip in range(chips)] for core in range(2)]
    received = lax.all_to_all(copies, "pore", 0, 0, axis_index_groups=groups, tiled=True)
    mine = jnp.sum(received, axis=0)
    return mine, permuted(mine, "pore", lambda i: i ^ 1)


def swapped_faces(even_face, odd_face):
    inner = permuted(even_face, "pore", lambda i: i ^ 1)
    devices = lax.axis_size("pore")
    outer = permuted(odd_face, "pore", lambda i: (((i + 1) % devices ^ 1) - 1) % devices)
    return inner, outer


def is_odd():
    return lax.axis_index("pore") % 2 == 1


def lane_gather(block, blocks, index):
    shape = block(0).shape
    low = jnp.broadcast_to(index & 127, shape)
    high = jnp.broadcast_to(index >> 7, shape)
    found = jnp.take_along_axis(block(0), low, axis=1)
    for h in range(1, blocks):
        found = jnp.where(high == h, jnp.take_along_axis(block(h), low, axis=1), found)
    return found


def halves(x):
    high = x.astype(BF16)
    low = (x - high.astype(F32)).astype(BF16)
    return high, low


def one_hot(index, value):
    rows = lax.broadcasted_iota(jnp.int32, (256, index.shape[1]), 0)
    return jnp.where(rows == (index & 255), value, 0.0).astype(BF16)


def page_table(values_ref, table_ref):
    for h in range(8):
        high, low = halves(values_ref[:, h * 256 : (h + 1) * 256])
        table_ref[h * 64 : h * 64 + 32, :] = high
        table_ref[h * 64 + 32 : h * 64 + 64, :] = low


def page_gather(table_ref, index):
    found = lax.dot_general(table_ref[...], one_hot(index, 1.0), NN, preferred_element_type=F32)
    pages = [found[h * 64 : h * 64 + 32] + found[h * 64 + 32 : h * 64 + 64] for h in range(8)]
    page = jnp.broadcast_to(index >> 8, pages[0].shape)
    picked = pages[0]
    for h in range(1, 8):
        picked = jnp.where(page == h, pages[h], picked)
    return picked


def spread(values, index):
    both = jnp.concatenate(halves(values), axis=0)
    page = index >> 8
    pages = []
    for h in range(8):
        pages.append(both * jnp.where(page == h, 1.0, 0.0).astype(BF16))
    return jnp.concatenate(pages, axis=0)


def page_value(acc_ref, h):
    return acc_ref[h * 64 : h * 64 + 32, :] + acc_ref[h * 64 + 32 : h * 64 + 64, :]


def tile_of(ref, first=0):
    rows = slice(first, first + BCOL)
    return lambda h: ref[rows, h * 128 : (h + 1) * 128]


def apply_inverse(source_ref, perm_ref, inverse_ref, acc_ref, out_ref):
    for chunk in range(4):
        parts = []
        for c in range(4 * chunk, 4 * chunk + 4):
            picked = lane_gather(tile_of(source_ref), 16, perm_ref[0:1, c * 128 : (c + 1) * 128])
            both = jnp.concatenate(halves(picked), axis=0)
            solved = lax.dot_general(both, inverse_ref[c], NN, preferred_element_type=F32)
            parts.append(solved[:BCOL] + solved[BCOL:])
        index = perm_ref[0:1, chunk * 512 : (chunk + 1) * 512]
        part = lax.dot_general(
            spread(jnp.concatenate(parts, axis=1), index),
            one_hot(index, 1.0),
            NT,
            preferred_element_type=F32,
        )
        if chunk == 0:
            acc_ref[...] = part
        else:
            acc_ref[...] += part
    for h in range(8):
        out_ref[:, h * 256 : (h + 1) * 256] = page_value(acc_ref, h)


def fill_sends(values_ref, blocks_ref, count_ref, send_refs, first=0):
    odd = jnp.where(is_odd(), 1, 0)
    rows = slice(first, first + values_ref.shape[0])
    place = lax.axis_index("pore")
    met = (place > 0) & (place < lax.axis_size("pore") - 1)
    for side, faced, send_ref in zip((1 - odd, odd), (True, met), send_refs):
        count = jnp.where(faced, count_ref[0, side], 0)
        for s in range(8):
            start = pl.multiple_of(blocks_ref[side, s] * 128, 128)
            live = jnp.where(s < count, 1.0, 0.0)
            send_ref[rows, s * 128 : (s + 1) * 128] = values_ref[:, pl.ds(start, 128)] * live


def start_kernel(
    blocks_hbm, count_hbm, ids_hbm, weight_hbm, rhs_hbm, perm_hbm, inverse_hbm,
    source_ref, smooth_ref, inner_ref, outer_ref,
    acc_ref, blocks_ref, count_ref, ids_ref, weight_ref, perm_ref, inverse_ref, sems,
):
    pairs = (
        (rhs_hbm, source_ref),
        (inverse_hbm, inverse_ref),
        (ids_hbm, ids_ref),
        (weight_hbm, weight_ref),
        (perm_hbm, perm_ref),
        (blocks_hbm, blocks_ref),
        (count_hbm, count_ref),
    )
    copies = [pltpu.make_async_copy(src, dst, sems.at[n]) for n, (src, dst) in enumerate(pairs)]
    for copy in copies:
        copy.start()
    for n, copy in enumerate(copies):
        if n != 1:
            copy.wait()
    first_pore = lax.axis_index("pore") * source_ref.shape[1]
    lanes = lax.broadcasted_iota(jnp.int32, (1, 128), 1)
    for f in range(BCOL):
        place = ids_ref[f] - first_pore
        inside = (place >= 0) & (place < source_ref.shape[1])
        place = jnp.where(inside, place, 0)
        tile = pl.ds(pl.multiple_of((place >> 7) * 128, 128), 128)
        added = jnp.where(inside, weight_ref[f], 0.0)
        source_ref[f : f + 1, tile] += jnp.where(lanes == (place & 127), added, 0.0)
    copies[1].wait()
    apply_inverse(source_ref, perm_ref, inverse_ref, acc_ref, smooth_ref)
    fill_sends(smooth_ref, blocks_ref, count_ref, (inner_ref, outer_ref))


def local_kernel(
    values_ref, ends_ref, cond_ref, shift_ref, out_ref, cross_ref, acc_ref, table_ref
):
    block = tile_of(values_ref)
    page_table(values_ref, table_ref)

    def flux_of(part):
        near = page_gather(table_ref, ends_ref[0:1, part])
        far = [
            lane_gather(block, 16, ends_ref[1:2, g : g + 128])
            for g in range(part.start, part.stop, 128)
        ]
        return (near - jnp.concatenate(far, axis=1)) * cond_ref[0:1, part]

    def scattered(flux, part):
        near = ends_ref[0:1, part]
        far = ends_ref[1:2, part]
        left = jnp.concatenate([spread(flux, near), spread(flux, far)], axis=1)
        right = jnp.concatenate([one_hot(near, 1.0), one_hot(far, -1.0)], axis=1)
        return lax.dot_general(left, right, NT, preferred_element_type=F32)

    parts = [slice(start, start + CHUNK) for start in range(0, 4096, CHUNK)]
    flux = flux_of(parts[0])
    for n, part in enumerate(parts):
        later = flux_of(parts[n + 1]) if n + 1 < len(parts) else None
        if n == 0:
            acc_ref[...] = scattered(flux, part)
        else:
            acc_ref[...] += scattered(flux, part)
        flux = later
    for start in range(0, 2048, CHUNK):
        index = ends_ref[0:1, 4096 + start : 4096 + start + CHUNK]
        cross_ref[:, start : start + CHUNK] = page_gather(table_ref, index)
    for h in range(8):
        part = slice(h * 256, (h + 1) * 256)
        out_ref[:, part] = shift_ref[0:1, part] * values_ref[:, part] + page_value(acc_ref, h)


def add_cross(
    partial_ref, cross_ref, inner_ref, outer_ref, ends_ref, cond_ref, acc_ref, face_ref, out_ref
):
    odd = is_odd()
    inner = inner_ref[:BCOL, :]
    outer = outer_ref[:BCOL, :]
    face_ref[0] = jnp.where(odd, inner, outer)
    face_ref[1] = jnp.where(odd, outer, inner)
    for chunk in range(4):
        ref, base = face_ref.at[chunk // 2], 2048 + chunk // 2 * 1024
        drops = []
        for g in range(4 * chunk, 4 * chunk + 4):
            part = slice(4096 + g * 128, 4096 + (g + 1) * 128)
            far = lane_gather(tile_of(ref), 8, ends_ref[1:2, part] - base)
            drops.append(cross_ref[:, g * 128 : (g + 1) * 128] - far)
        part = slice(4096 + chunk * 512, 4096 + (chunk + 1) * 512)
        near = ends_ref[0:1, part]
        flux = jnp.concatenate(drops, axis=1) * cond_ref[0:1, part]
        product = lax.dot_general(
            spread(flux, near), one_hot(near, 1.0), NT, preferred_element_type=F32
        )
        if chunk == 0:
            acc_ref[...] = product
        else:
            acc_ref[...] += product
    for h in range(8):
        part = slice(h * 256, (h + 1) * 256)
        out_ref[:, part] = partial_ref[:, part] + page_value(acc_ref, h)


def step_kernel(
    blocks_ref, count_ref, partial_ref, cross_ref, inner_ref, outer_ref, ends_ref, cond_ref,
    perm_ref, inverse_ref, mapped_ref, smooth_ref, inner_send, outer_send, acc_ref, face_ref,
):
    add_cross(
        partial_ref, cross_ref, inner_ref, outer_ref, ends_ref, cond_ref, acc_ref, face_ref, mapped_ref
    )
    apply_inverse(mapped_ref, perm_ref, inverse_ref, acc_ref, smooth_ref)
    fill_sends(smooth_ref, blocks_ref, count_ref, (inner_send, outer_send))


def first_step_kernel(blocks_ref, count_ref, pressure_ref, *refs):
    step_kernel(blocks_ref, count_ref, *refs)
    sends = refs[10:12]
    for ref in sends:
        ref[BCOL:, :] = jnp.zeros((8, 1024), F32)
    fill_sends(pressure_ref, blocks_ref, count_ref, sends, BCOL)


def exact_dot(a, b, dims):
    return lax.dot_general(a, b, dims, precision=lax.Precision.HIGHEST, preferred_element_type=F32)


def square_index():
    return (lax.broadcasted_iota(jnp.int32, (BCOL, BCOL), axis) for axis in (0, 1))


def packed(moments):
    row, column = square_index()
    pairs, diagonals = [], []
    for upper, lower in zip(moments[::2], moments[1::2]):
        pairs.append(jnp.where(row <= column, upper, lower))
        diagonals.append(jnp.sum(jnp.where(row == column, lower, 0.0), axis=0, keepdims=True))
    diagonals.append(jnp.zeros((BCOL - 3, BCOL), F32))
    return jnp.concatenate(pairs + [jnp.concatenate(diagonals, axis=0)], axis=1)


def unpacked(table):
    row, column = square_index()
    turned = table.T
    moments = []
    for n in range(3):
        pair = table[:, BCOL * n : BCOL * (n + 1)]
        mirror = turned[BCOL * n : BCOL * (n + 1), :]
        diagonal = table[n : n + 1, 3 * BCOL :]
        moments.append(jnp.where(row <= column, pair, mirror))
        outside = jnp.where(row > column, pair, mirror)
        moments.append(jnp.where(row == column, diagonal, outside))
    return moments


def last_kernel(
    partial_ref, cross_ref, inner_ref, outer_ref, ends_ref, cond_ref,
    z0_ref, z1_ref, z2_ref, q0_ref, q1_ref, source_ref, mapped_ref, moment_ref, acc_ref, face_ref,
):
    add_cross(
        partial_ref, cross_ref, inner_ref, outer_ref, ends_ref, cond_ref, acc_ref, face_ref, mapped_ref
    )
    smooth = jnp.concatenate([z0_ref[...], z1_ref[...], z2_ref[...]], axis=0)
    mapped = jnp.concatenate([q0_ref[...], q1_ref[...], mapped_ref[...], source_ref[...]], axis=0)
    products = lax.dot_general(
        jnp.concatenate(halves(smooth), axis=0),
        jnp.concatenate(halves(mapped), axis=0),
        NT,
        preferred_element_type=F32,
    )
    gram = products[:96] + products[96:]
    gram = gram[:, :128] + gram[:, 128:]
    z0, z1, z2 = gram[:32], gram[32:64], gram[64:]
    moments = packed(
        (z0[:, 96:], z0[:, :32], z1[:, :32], z1[:, 32:64], z2[:, 32:64], z2[:, 64:96])
    )
    for n in range(moment_ref.shape[0]):
        moment_ref[n] = moments


def solved_block(block, start):
    tiles = [block[8 * v : 8 * v + 8, :] for v in range(4)]
    row_at = lax.broadcasted_iota(jnp.int32, (8, 128), 0)
    for first in range(0, 8 * 4, SIDE):
        columns = [
            [
                jnp.broadcast_to(tile[:, start + first + p : start + first + p + 1], (8, 128))
                for p in range(SIDE)
            ]
            for tile in tiles
        ]
        own = range(first // 8, (first + SIDE) // 8)
        pivots = {u: list(columns[u]) for u in own}
        solved = {u: tiles[u] for u in own}
        for p in range(SIDE):
            v, r = divmod(first + p, 8)
            inverse = 1.0 / pivots[v][p][r : r + 1, :]
            row = solved[v][r : r + 1, :] * inverse
            factors = [pivots[v][q][r : r + 1, :] * inverse for q in range(p + 1, SIDE)]
            for u in own:
                solved[u] = solved[u] - pivots[u][p] * row
                for q, factor in zip(range(p + 1, SIDE), factors):
                    pivots[u][q] = pivots[u][q] - pivots[u][p] * factor
            solved[v] = jnp.where(row_at == r, row, solved[v])
            for q, factor in zip(range(p + 1, SIDE), factors):
                pivots[v][q] = jnp.where(row_at == r, factor, pivots[v][q])
        for u in range(4):
            if u in own:
                tiles[u] = solved[u]
                continue
            products = [
                columns[u][p] * solved[(first + p) // 8][p % 8 : p % 8 + 1, :] for p in range(SIDE)
            ]
            while len(products) > 1:
                products = [a + b for a, b in zip(products[::2], products[1::2])]
            tiles[u] = tiles[u] - products[0]
    return jnp.concatenate(tiles, axis=0)


def solved_table(table):
    size = 8 * 4
    for first in range(0, 96, size):
        solved = solved_block(table[first : first + size, :], first)
        table = table - exact_dot(table[:, first : first + size], solved, NN)
        parts = [table[:first], solved, table[first + size :]]
        table = jnp.concatenate([part for part in parts if part.shape[0]], axis=0)
    return [table[8 * v : 8 * v + 8, :] for v in range(12)]


def ends_tile(ends_ref, end, v):
    rows = [ends_ref[end : end + 1, j * 128 : (j + 1) * 128] for j in range(8 * v, 8 * v + 8)]
    return jnp.concatenate(rows, axis=0)


def throat_drop(row_ref, ends_ref, v):
    def block_at(offset):
        return lambda h: row_ref[:, offset + h * 128 : offset + (h + 1) * 128]

    offset, blocks = ((0, 16), (2048, 8), (3072, 8))[max(v - 3, 0)]
    near = lane_gather(block_at(0), 16, ends_tile(ends_ref, 0, v))
    return near - lane_gather(block_at(offset), blocks, ends_tile(ends_ref, 1, v) - offset)


def place_faces(row_ref, inner, outer):
    odd = is_odd()
    row_ref[:, 2048:3072] = jnp.broadcast_to(jnp.where(odd, inner, outer), (8, 1024))
    row_ref[:, 3072:4096] = jnp.broadcast_to(jnp.where(odd, outer, inner), (8, 1024))


def pressure_kernel(pressure_ref, inner_ref, outer_ref, ends_ref, drop_ref, row_ref):
    row_ref[:, 0:2048] = jnp.broadcast_to(pressure_ref[0:1, :], (8, 2048))
    place_faces(row_ref, inner_ref[BCOL : BCOL + 1, :], outer_ref[BCOL : BCOL + 1, :])
    for v in range(6):
        drop = throat_drop(row_ref, ends_ref, v)
        drop_ref[8 * v : 8 * v + 8, :] = drop * (-1.0 / math.sqrt(FIELDS))


def solve_kernel(
    mine_ref, other_ref, z0_ref, z1_ref, z2_ref, i0_ref, i1_ref, i2_ref, o0_ref, o1_ref, o2_ref,
    drop_ref, ends_ref, coeff_ref, term_ref, row_ref, total_ref,
):
    m = unpacked(mine_ref[...] + other_ref[...])
    rows = [jnp.concatenate([m[n + 1], m[n + 2], m[n + 3], m[n]], axis=1) for n in range(3)]
    tiles = solved_table(jnp.concatenate(rows, axis=0))
    for v in range(12):
        coeff_ref[8 * v : 8 * v + 8, :] = tiles[v][:, 96:]
    weights = [
        jnp.broadcast_to(jnp.sum(tile[:, 96:], axis=1, keepdims=True), (8, 128)) for tile in tiles
    ]

    def weighted(refs, start):
        part = slice(start, start + 128)
        total = None
        for v in range(12):
            ref = refs[v // 4]
            product = weights[v] * ref[8 * (v % 4) : 8 * (v % 4) + 8, part]
            total = product if total is None else total + product
        return jnp.sum(total, axis=0, keepdims=True)

    for start in range(0, 2048, 128):
        row_ref[:, start : start + 128] = jnp.broadcast_to(
            weighted((z0_ref, z1_ref, z2_ref), start), (8, 128)
        )
    inner, outer = (
        jnp.concatenate([weighted(refs, start) for start in range(0, 1024, 128)], axis=1)
        for refs in ((i0_ref, i1_ref, i2_ref), (o0_ref, o1_ref, o2_ref))
    )
    place_faces(row_ref, inner, outer)
    for v in range(6):
        drop = throat_drop(row_ref, ends_ref, v)
        total_ref[8 * v : 8 * v + 8, :] = drop * drop_ref[8 * v : 8 * v + 8, :]
    for n in range(8):
        term_ref[n] = total_ref[6 * n : 6 * n + 6, :]


def finish_kernel(
    coeff_ref, z0_ref, z1_ref, z2_ref, q0_ref, q1_ref, q2_ref, source_ref, adjoint_ref, residual_ref
):
    coeff = coeff_ref[...]
    smooth = jnp.concatenate([z0_ref[...], z1_ref[...], z2_ref[...]], axis=0)
    mapped = jnp.concatenate([q0_ref[...], q1_ref[...], q2_ref[...]], axis=0)
    adjoint_ref[...] = exact_dot(coeff, smooth, TN)
    residual_ref[...] = source_ref[...] - exact_dot(coeff, mapped, TN)


def call(kernel, spaces, args, outs, scratch, name, flops=0, limit=32 << 10):
    return pl.pallas_call(
        kernel,
        out_shape=[jax.ShapeDtypeStruct(s, F32) for s in outs],
        in_specs=[pl.BlockSpec(memory_space=space) for space in spaces],
        out_specs=[pl.BlockSpec(memory_space=pltpu.VMEM)] * len(outs),
        scratch_shapes=scratch,
        compiler_params=pltpu.CompilerParams(vmem_limit_bytes=limit << 10),
        cost_estimate=pl.CostEstimate(flops=flops, bytes_accessed=2 << 20, transcendentals=0),
        name=name,
    )(*args)


def shards(
    rhs, well_ids, well_weight, pressure, shift, conductance, throat_ends, boundary_blocks,
    boundary_count, jacobi_perm, jacobi_inverse,
):
    pores = rhs.shape[1]
    perm = jacobi_perm[None, :]
    pressure_row = pressure[None, :]
    shift_row = shift[None, :]
    cond = conductance[None, :]
    field = (BCOL, pores)
    sent = (BCOL, 1024)
    smem, vmem = pltpu.SMEM, pltpu.VMEM
    acc = pltpu.VMEM((512, 256), F32)
    table = pltpu.VMEM((512, 256), BF16)
    face = pltpu.VMEM((2, *sent), F32)
    work = 12 * 10**9

    counts = boundary_count.T
    chips = lax.axis_size("pore") // 2
    source, z, *sends = call(
        start_kernel, [pltpu.HBM] * 7,
        (boundary_blocks, counts, well_ids, well_weight, rhs, perm, jacobi_inverse),
        (field, field, sent, sent),
        [
            acc, smem(boundary_blocks.shape, jnp.int32), smem(counts.shape, jnp.int32),
            smem(well_ids.shape, jnp.int32), smem(well_weight.shape, F32),
            vmem(perm.shape, jnp.int32), vmem(jacobi_inverse.shape, BF16),
            pltpu.SemaphoreType.DMA((7,)),
        ],
        "start", limit=53 << 10,
    )
    smooths, mappeds, inners, outers = [], [], [], []
    for k in range(ITERS):
        inner, outer = swapped_faces(*sends)
        partial, cross = call(
            local_kernel, [vmem] * 4, (z, throat_ends, cond, shift_row),
            (field, field), [acc, table], "local", work,
        )
        smooths.append(z)
        inners.append(inner)
        outers.append(outer)
        met = (partial, cross, inner, outer, throat_ends, cond)
        if k + 1 < ITERS:
            extra = (pressure_row,) if k == 0 else ()
            faces = (BCOL + 8 * len(extra), 1024)
            mapped, z, *sends = call(
                step_kernel if k else first_step_kernel, [smem] * 2 + [vmem] * (8 + len(extra)),
                (boundary_blocks, counts, *extra, *met, perm, jacobi_inverse),
                (field, field, faces, faces), [acc, face], "step",
            )
        else:
            mapped, moments = call(
                last_kernel, [vmem] * 12, met + (*smooths, *mappeds, source),
                (field, (chips, BCOL, 128)), [acc, face], "last",
            )
        mappeds.append(mapped)
    mine, other = pore_sum(moments)
    row = pltpu.VMEM((8, 4096), F32)
    (drop,) = call(
        pressure_kernel, [vmem] * 4, (pressure_row, inners[1], outers[1], throat_ends),
        ((48, 128),), [row], "pressure", work,
    )
    coeff, term = call(
        solve_kernel, [vmem] * 13, (mine, other, *smooths, *inners, *outers, drop, throat_ends),
        ((96, BCOL), (8, 6, 128)), [row, pltpu.VMEM((48, 128), F32)], "solve",
    )
    shared = lax.all_to_all(term, "field", 0, 0, tiled=True)
    adjoint, residual = call(
        finish_kernel, [vmem] * 8, (coeff, *smooths, *mappeds, source), (field, field), [],
        "finish", work,
    )
    gradient = jnp.sum(shared, axis=0).reshape(-1)
    return (adjoint, residual, gradient)


def solution(mesh):
    in_specs = (
        P("field", "pore"),
        P("field"),
        P("field"),
        P("pore"),
        P("pore"),
        P("pore"),
        P(None, "pore"),
        P(None, "pore"),
        P(None, "pore"),
        P("pore"),
        P("pore", None, None),
    )
    out_specs = (P("field", "pore"), P("field", "pore"), P(("pore", "field")))
    return jax.shard_map(shards, mesh=mesh, in_specs=in_specs, out_specs=out_specs, check_vma=False)
```
